256 devices in a mesh: expert: 8 (over z), shard: 32 (over y, x, core).
Axes of the slice: x: 4, y: 4, z: 8, core: 2. Of those that a mesh axis runs over, the one named last changes fastest.
Arguments:
- tokens: bfloat16 [256, 6144], P('expert'), may hold values from -6 to 6
- routes: int32 [256, 2], P('expert'), may hold values from 0 to 7, all different within a row; in each aligned block of 32 rows (0 to 31, 32 to 63, ...) at most 16 rows name the same one
- router_logits: float32 [256, 2], P('expert'), may hold values from -6 to 6
- gate_weight: bfloat16 [8, 6144, 8192], P('expert', None, 'shard'), may hold values from -0.078125 to 0.078125
- up_weight: bfloat16 [8, 6144, 8192], P('expert', None, 'shard'), may hold values from -0.078125 to 0.078125
- down_weight: bfloat16 [8, 8192, 4096], P('expert', 'shard'), may hold values from -6 to 6
- kept_blocks: int32 [8, 64, 32], P('expert', 'shard'), may hold values 0 or 1
Outputs:
- refit_out: bfloat16 [256, 4096], P('expert', 'shard')
- new_down: bfloat16 [8, 8192, 4096], P('expert', 'shard')
The draws below stay inside these ranges and needn't reach their ends.
Inputs may be any that keep to these rules, and one draw needn't show every extreme that they name: `routes`: within the 32 rows of one owning group, each expert is named by at most 16 picks, a bound that some block reaches; the two picks of a row differ.
All inputs are finite; a program needn't handle non-finite values. No bound on the sum of `kept_blocks` on one device may be relied on, other than what follows from the above.
Results may differ from the reference program's by a relative error of at most 0.024.
Values may be sent and summed in bfloat16 or wider, within the bound.
A program may use at most 128 MiB of HBM per device.

```python
import math
import jax
import jax.numpy as jnp
import numpy as np
from jax import lax

D = 6144
FF = 8192
DW = 4096
BLOCK = 128
ITERS = 3
TOK_DEV = 32
EXPERTS = 8
CAP = 16
TOKENS = 256
N_EXPERT = 8


def set_ends(result, key, least, high):
    dims = result.shape
    index_at = [jax.random.randint(jax.random.fold_in(key, axis), (), 0, dims[axis]) for axis in range(len(dims))]
    result = result.at[tuple(index_at)].set(least)
    longest = dims.index(max(dims))
    index_at[longest] = (index_at[longest] + 1) % dims[longest]
    return result.at[tuple(index_at)].set(high)


def steps_of(stream_key, extent, shards, low, largest):
    def one(axis_at, shards_of):
        draws = jax.random.uniform(jax.random.fold_in(jax.random.fold_in(stream_key, 6), axis_at), (shards_of,), jnp.float32, low / len(shards), largest / len(shards))
        return jnp.repeat(jnp.exp(draws), extent[axis_at] // shards_of).reshape((-1,) + (1,) * (len(extent) - axis_at - 1))

    loudness = one(*shards[0])
    for cut in shards[1:]:
        loudness = loudness * one(*cut)
    return loudness


def deal_out(stream_key, own, number, rows, amount, top, bound, lean):
    ranking = jax.random.permutation(stream_key, amount)
    packed, ordinary = load_shares(amount, rows * top, bound, lean, True), load_shares(amount, rows * top, bound, lean, False)
    places = jnp.arange(amount)

    def named(tallies, offset_by):
        used = int((tallies > 0).sum())
        fixed = max(1, used // 4)
        moved = fixed + (places - fixed + offset_by * (used - fixed)) % max(1, amount - fixed)
        return jnp.zeros((amount,), jnp.int32).at[ranking[jnp.where(places < fixed, places, moved)]].set(jnp.asarray(tallies, jnp.int32))

    tallies = jnp.where(number % 4 == 0, named(packed, number // 4), named(ordinary, number - number // 4 - 1))
    mixed = jax.random.permutation(jax.random.fold_in(own, 3), amount)
    donor, sink = mixed[0:amount // 2 * 2:2], mixed[1:amount // 2 * 2:2]
    margin = jnp.minimum(tallies[donor] - 1, bound - tallies[sink]) // 2
    margin = jnp.where((donor == ranking[0]) | (sink == ranking[0]) | (tallies[sink] == 0), 0, jnp.maximum(margin, 0))
    moved = jax.random.randint(jax.random.fold_in(own, 4), (amount // 2,), 0, 1 << 20) % (margin + 1)
    tallies = tallies.at[donor].add(-moved).at[sink].add(moved)
    labels = jnp.searchsorted(jnp.cumsum(tallies), jnp.arange(rows * top), side="right").astype(jnp.int32)
    listing = labels.reshape(top, rows).T
    listing = listing[jax.random.permutation(jax.random.fold_in(own, 1), rows)]
    offset_by = jax.random.randint(jax.random.fold_in(own, 2), (rows, 1), 0, top)
    return jnp.take_along_axis(listing, (jnp.arange(top)[None, :] + offset_by) % top, axis=1)


def load_shares(number_of, total, bound, slope, full):
    weights = [(1 << 20) // math.isqrt(standing ** slope) + 1 for standing in range(1, number_of + 1)]
    largest = bound if full else min(bound, max(-(-total // number_of), total * weights[0] // sum(weights)))
    least = 1 if total - largest >= number_of - 1 else 0
    counts, rest = [largest] + [least] * (number_of - 1), total - largest - least * (number_of - 1)
    while rest > 0:
        free = [i for i in range(1, number_of) if counts[i] < largest] or [i for i in range(1, number_of) if counts[i] < bound]
        pool, left = sum([weights[i] for i in free]), rest
        for i in free:
            extra = min(bound - counts[i], max(1, left * weights[i] // pool), rest)
            counts[i] = counts[i] + extra
            rest = rest - extra
    return np.array(counts)


def normal_values(own_key, shape, scale, reach, pieces=(), kind=jnp.bfloat16):
    result = jax.random.normal(own_key, shape, jnp.float32) * scale
    if len(pieces) > 0:
        result = steps_of(own_key, shape, pieces, -0.22, 0.18) * result
    return jnp.clip(result, min=-reach, max=reach).astype(kind)


def setup_inputs(seed: int = 0) -> dict:
    arg_keys = jax.random.split(jax.random.key(seed), 8)
    tokens = normal_values(arg_keys[0], (TOKENS, D), 1.0, 6.0, ((0, 8),))
    routes_keys = jax.random.split(jax.random.fold_in(arg_keys[1], 1), TOKENS // TOK_DEV)
    routes_turns = jax.random.permutation(jax.random.fold_in(arg_keys[1], 3), TOKENS // TOK_DEV)
    routes = jax.vmap(lambda own, number: deal_out(jax.random.fold_in(arg_keys[1], 2), own, number, TOK_DEV, EXPERTS, 2, CAP, 2))(routes_keys, routes_turns).reshape((TOKENS, 2))
    router_logits = normal_values(arg_keys[2], (TOKENS, 2), 1.5, 6.0, ((0, 8),), jnp.float32)
    gate_weight = normal_values(arg_keys[3], (EXPERTS, D, FF), D ** -0.5, 0.078125, ((0, 8), (2, 32)))
    up_weight = normal_values(arg_keys[4], (EXPERTS, D, FF), D ** -0.5, 0.078125, ((0, 8), (2, 32)))
    down_weight = normal_values(arg_keys[5], (EXPERTS, FF, DW), 1.0, 6.0, ((0, 8), (1, 32)))
    kept_blocks = set_ends((jax.random.randint(arg_keys[6], (EXPERTS, FF // BLOCK, DW // BLOCK), 0, 5) < 3).astype(jnp.int32), jax.random.fold_in(arg_keys[6], 1), 0, 1)
    return {"tokens": tokens, "routes": routes, "router_logits": router_logits, "gate_weight": gate_weight, "up_weight": up_weight, "down_weight": down_weight, "kept_blocks": kept_blocks}


epsilon = 1e-6


def expand_mask(blocks, block_edge):
    row_blocks, col_blocks = blocks.shape
    spread = jnp.broadcast_to(blocks[:, None, :, None], (row_blocks, block_edge, col_blocks, block_edge))
    return spread.reshape(row_blocks * block_edge, col_blocks * block_edge).astype(jnp.float32)


def slot_targets(routes, experts, capacity):
    chosen = routes.reshape(-1)
    onehot = (chosen[:, None] == jnp.arange(experts, dtype=jnp.int32)[None, :]).astype(jnp.int32)
    before = jnp.cumsum(onehot, axis=0) - onehot
    slot_rank = jnp.sum(before * onehot, axis=1)
    return (chosen * capacity + slot_rank).reshape(routes.shape)


def refit_expert(hidden, initial, keep_mask):
    factor = FF ** -0.5
    highest = lax.Precision.HIGHEST
    hidden_wide = hidden.astype(jnp.float32)

    def forward(operand):
        return factor * jnp.dot(hidden_wide, operand, precision=highest)

    def adjoint(operand):
        return keep_mask * (factor * jnp.dot(hidden_wide.T, operand, precision=highest))

    weights = keep_mask * initial
    residual = forward(initial - weights)
    gradient = adjoint(residual)
    direction = gradient
    grad_norm = jnp.sum(gradient * gradient)
    for iteration in range(ITERS):
        image_cols = forward(direction)
        step_size = grad_norm / (jnp.sum(image_cols * image_cols) + epsilon)
        weights = weights + step_size * direction
        residual = residual - step_size * image_cols
        gradient = adjoint(residual)
        new_norm = jnp.sum(gradient * gradient)
        direction = gradient + (new_norm / (grad_norm + epsilon)) * direction
        grad_norm = new_norm
    return weights, forward(weights).astype(jnp.bfloat16)


def reference(tokens, routes, router_logits, gate_weight, up_weight, down_weight, kept_blocks):
    local_routes = routes.reshape(N_EXPERT, TOK_DEV, 2)
    targets = jax.vmap(lambda block_routes: slot_targets(block_routes, EXPERTS, CAP))(local_routes)
    sources = jnp.arange(N_EXPERT, dtype=jnp.int32)[:, None, None]
    row_index = (sources * CAP + targets - local_routes * CAP).reshape(-1).astype(jnp.int32)
    expert_index = local_routes.reshape(-1).astype(jnp.int32)
    repeated = jnp.repeat(tokens, 2, axis=0)
    dispatched = jnp.zeros((EXPERTS, N_EXPERT * CAP, D), jnp.bfloat16).at[expert_index, row_index].set(repeated)
    new_down = []
    fitted = []
    for expert in range(EXPERTS):
        gate_act = jnp.dot(dispatched[expert], gate_weight[expert], preferred_element_type=jnp.float32)
        up_act = jnp.dot(dispatched[expert], up_weight[expert], preferred_element_type=jnp.float32)
        hidden = (jax.nn.silu(gate_act) * up_act).astype(jnp.bfloat16)
        keep_mask = expand_mask(kept_blocks[expert], BLOCK)
        weights, fitted_rows = refit_expert(hidden, down_weight[expert].astype(jnp.float32), keep_mask)
        new_down.append(weights.astype(jnp.bfloat16))
        fitted.append(fitted_rows)
    fitted = jnp.stack(fitted)
    picked = fitted[expert_index, row_index].astype(jnp.float32).reshape(N_EXPERT * TOK_DEV, 2, DW)
    first_share = jax.nn.sigmoid(router_logits[:, 0] - router_logits[:, 1])
    shares = jnp.stack([first_share, 1.0 - first_share], axis=1)
    refit_out = jnp.sum(shares[:, :, None] * picked, axis=1).astype(jnp.bfloat16)
    return (refit_out, jnp.stack(new_down))
```

```python
import functools

import jax
import jax.numpy as jnp
from jax import lax
from jax.experimental import pallas as pl
from jax.experimental.pallas import tpu as pltpu
from jax.sharding import PartitionSpec as P

FF = 8192
DW = 4096
EPS = 1e-6
FACTOR = FF ** -0.5
CAP = 16
GROUPS = 8
CHIPS = 16
SHARDS = 32
ROWS = GROUPS * CAP
TINY = 1e-30
MESH = pl.DeviceIdType.MESH
F32 = jnp.float32
BF16 = jnp.bfloat16

ORDER = (1, 3, 5, 7, 0, 2, 4, 6)


def dot(a, b, ca=1, cb=0):
    return lax.dot_general(a, b, (((ca,), (cb,)), ((), ())), preferred_element_type=F32)


def slot_columns(routes_ref, plane):
    rel = [lax.rem(routes_ref[:, k:k + 1] - plane + GROUPS, GROUPS) for k in range(2)]
    tok = rel[0].shape[0]
    lanes = lax.broadcasted_iota(jnp.int32, (tok, 128), 1)
    onehot = [(r == lanes).astype(F32) for r in rel]
    lower = lax.broadcasted_iota(jnp.int32, (tok, tok), 1) < lax.broadcasted_iota(jnp.int32, (tok, tok), 0)
    before = dot(lower.astype(BF16), (onehot[0] + onehot[1]).astype(BF16))
    slots = [jnp.sum(before * o, axis=1, keepdims=True) for o in onehot]
    return [((r * CAP).astype(F32) + s == lanes.astype(F32)) for r, s in zip(rel, slots)]


def step_scalars(m, eps1, eps2):
    def form(p, shift):
        total = None
        size = None
        for i, a in enumerate(p):
            for j, b in enumerate(p):
                term = a * b * m[i + j + shift]
                total = term if total is None else total + term
                size = jnp.abs(term) if size is None else size + jnp.abs(term)
        return jnp.maximum(total, 0.0), size

    one = jnp.ones_like(m[1])
    r, s = [one], [one]
    gnorm, _ = form(r, 1)
    out = None
    for it in range(3):
        image, size = form(s, 2)
        image = jnp.maximum(image, 1e-6 * size)
        step = gnorm / (image + eps2)
        term = [step * a for a in s]
        out = term if out is None else [a + b for a, b in zip(out + [0.0] * (len(term) - len(out)), term)]
        if it < 2:
            r = [a - b for a, b in zip(r + [0.0], [0.0] + term)]
            fresh, _ = form(r, 1)
            beta = fresh / (gnorm + eps1)
            s = [a + b for a, b in zip(r, [beta * c for c in s] + [0.0])]
            gnorm = fresh
    return out


def kernel(tok_hbm, routes_ref, logits_ref, gate_hbm, up_hbm, down_hbm, kept_ref,
           refit_ref, new_ref,
           tok, gate, up, down, outgoing, xg, acc_g, acc_u, hown, hsib, ht, vsib, kb, ksib, gram,
           stage, rs, av, tiles, sg, fit, ret,
           load_sem, z_ssem, z_rsem, ag_ssem, ag_rsem, fw_ssem, fw_rsem, v_ssem, v_rsem, k_sem, h_sem,
           rs_ssem, rs_rsem, av_ssem, av_rsem, t_ssem, t_rsem, s_ssem, s_rsem, sf_ssem, sf_rsem, r_ssem, r_rsem):
    e = lax.axis_index("expert")
    s = lax.axis_index("shard")
    p = s // 2
    c = lax.rem(s, 2)
    sib = (e, 2 * p + 1 - c)
    width = tok.shape[1]

    def chip(k):
        return lax.rem(p + k, CHIPS)

    def from_chip(k):
        return lax.rem(p + CHIPS - k, CHIPS)

    def plane(d):
        return lax.rem(e + d, GROUPS)

    def back(d):
        return lax.rem(e + GROUPS - d, GROUPS)

    def remote(src, dst, ssem, rsem, device):
        return pltpu.make_async_remote_copy(src_ref=src, dst_ref=dst, send_sem=ssem, recv_sem=rsem,
                                            device_id=device, device_id_type=MESH)

    def loop(lo, hi, f):
        lax.fori_loop(lo, hi, lambda k, _: (f(k), 0)[1], 0)

    barrier = pltpu.get_barrier_semaphore()
    loop(1, GROUPS, lambda d: pl.semaphore_signal(barrier, inc=1, device_id=(plane(d), s), device_id_type=MESH))
    loop(1, SHARDS, lambda k: pl.semaphore_signal(barrier, inc=1, device_id=(e, lax.rem(s + k, SHARDS)), device_id_type=MESH))

    loads = [
        pltpu.make_async_copy(tok_hbm.at[:, pl.ds(pl.multiple_of(p * width, 128), width)], tok, load_sem.at[0]),
        pltpu.make_async_copy(gate_hbm.at[0], gate, load_sem.at[1]),
        pltpu.make_async_copy(up_hbm.at[0], up, load_sem.at[2]),
        pltpu.make_async_copy(down_hbm.at[0], down, load_sem.at[3]),
    ]
    for load in loads:
        load.start()

    match = slot_columns(routes_ref, e)
    logit = logits_ref[:, 0:1] - logits_ref[:, 1:2]
    share = 1.0 / (1.0 + jnp.exp(-logit))
    combining = jnp.where(match[0], share, 0.0) + jnp.where(match[1], 1.0 - share, 0.0)
    kept = kept_ref[0].astype(F32)
    row = lax.broadcasted_iota(jnp.int32, (2, 128), 0)
    for f in range(2):
        kb[f] = dot(kept, (row == f).astype(F32), 0, 0)
    loads[0].wait()
    placing = (match[0] | match[1]).astype(BF16)
    outgoing[...] = dot(placing, tok[...], 0, 0).astype(BF16)

    pl.semaphore_wait(barrier, GROUPS - 1 + SHARDS - 1)

    def z_copy(i):
        d = 2 * i + 1 - c
        return remote(outgoing.at[pl.ds(pl.multiple_of(d * CAP, CAP), CAP)],
                      xg.at[p, c, pl.ds(pl.multiple_of(i * CAP, CAP), CAP)],
                      z_ssem.at[i], z_rsem.at[i], (plane(d), s))

    @pl.when(c == 0)
    def _():
        z_copy(0).start()

    @pl.when(c == 1)
    def _():
        xg[p, 1, 0:CAP] = outgoing[0:CAP]

    loop(1, 4, lambda i: z_copy(i).start())

    def v_copy(q):
        return remote(down_hbm.at[0, :, pl.ds(pl.multiple_of((2 * q + 1 - c) * 128, 128), 128)], vsib.at[q],
                      v_ssem.at[q], v_rsem.at[q], sib)

    loop(0, CHIPS, lambda q: v_copy(q).start())
    k_copy = remote(kb, ksib, k_sem.at[0], k_sem.at[1], sib)
    k_copy.start()

    @pl.when(c == 0)
    def _():
        z_copy(0).wait_recv()

    loop(1, 4, lambda i: z_copy(i).wait_recv())

    def ag_copy(k, q):
        return remote(xg.at[q, c], xg.at[q, c], ag_ssem.at[k], ag_rsem.at[k], (e, 2 * chip(k) + c))

    def fw_copy(k, q):
        return remote(xg.at[q, c], xg.at[q, c], fw_ssem.at[k], fw_rsem.at[k], sib)

    def fw_wait(k, q):
        remote(xg.at[q, 1 - c], xg.at[q, 1 - c], fw_ssem.at[k], fw_rsem.at[k], sib).wait_recv()

    loop(1, CHIPS, lambda k: ag_copy(k, p).start())
    fw_copy(0, p).start()
    for load in loads[1:]:
        load.wait()
    acc_g[...] = jnp.zeros_like(acc_g)
    acc_u[...] = jnp.zeros_like(acc_u)

    def expand(k):
        q = from_chip(k)
        fw_wait(k, q)
        x = xg[q].reshape(ROWS, width)
        rows = pl.ds(pl.multiple_of(q * width, 128), width)
        acc_g[...] += dot(x, gate[rows, :])
        acc_u[...] += dot(x, up[rows, :])

    def gather_step(k):
        q = from_chip(k)
        ag_copy(k, q).wait_recv()
        fw_copy(k, q).start()
        expand(k - 1)

    loop(1, CHIPS, gather_step)
    expand(CHIPS - 1)

    g = acc_g[...]
    h32 = g / (1.0 + jnp.exp(-g)) * acc_u[...]
    hown[...] = h32.astype(BF16)
    h_copy = remote(hown, hsib, h_sem.at[0], h_sem.at[1], sib)
    h_copy.start()
    ht[...] = jnp.transpose(hown[...].astype(F32)).astype(BF16)

    def grams(h, base):
        for f in range(2):
            hf = h[:, f * 128:(f + 1) * 128]
            gram[base + f] = FACTOR * FACTOR * dot(hf, hf, 1, 1)

    grams(hown[...], 0)
    loop(0, CHIPS, lambda q: v_copy(q).wait_recv())
    k_copy.wait()
    h_copy.wait()
    grams(hsib[...], 2)

    def masked(v, k0, k1):
        return jnp.concatenate([v[:128] * (1.0 - k0).astype(BF16), v[128:] * (1.0 - k1).astype(BF16)], axis=0)

    def rs_copy(k, q):
        return remote(stage.at[q, pl.ds(0, 2)], rs.at[p], rs_ssem.at[k], rs_rsem.at[k], (e, 2 * q + c))

    def av_copy(k, q):
        return remote(stage.at[q, 2], av.at[p], av_ssem.at[k], av_rsem.at[k], (e, 2 * q + c))

    def partial(q):
        j = 2 * q + c
        ko = [kb[f, pl.ds(j, 1), :] for f in range(2)]
        ks = [ksib[f, pl.ds(j, 1), :] for f in range(2)]
        stage[q, 0] = (ko[0] * gram[0] + ko[1] * gram[1] + ks[0] * gram[2] + ks[1] * gram[3]).astype(BF16)
        vo = down[:, pl.ds(pl.multiple_of(j * 128, 128), 128)]
        vs = vsib[q]
        both = dot(hown[...], jnp.concatenate([masked(vo, *ko), vo], axis=1))
        both += dot(hsib[...], jnp.concatenate([masked(vs, *ks), vs], axis=1))
        both = (FACTOR * both).astype(BF16)
        stage[q, 1] = both[:, :128]
        stage[q, 2] = both[:, 128:]

    def send_partial(k):
        q = chip(k)
        partial(q)
        rs_copy(k, q).start()

    loop(1, CHIPS, send_partial)
    loop(1, CHIPS, lambda k: av_copy(k, chip(k)).start())
    partial(p)

    def add_up(k, carry):
        q = from_chip(k)
        remote(stage.at[p, pl.ds(0, 2)], rs.at[q], rs_ssem.at[k], rs_rsem.at[k], (e, 2 * q + c)).wait_recv()
        return carry[0] + rs[q, 0].astype(F32), carry[1] + rs[q, 1].astype(F32)

    big, r0 = lax.fori_loop(1, CHIPS, add_up, (stage[p, 0].astype(F32), stage[p, 1].astype(F32)))

    eye = lax.broadcasted_iota(jnp.int32, (128, 128), 0) == lax.broadcasted_iota(jnp.int32, (128, 128), 1)
    scale = jnp.sum(jnp.sum(jnp.where(eye, big, 0.0), axis=0, keepdims=True), axis=1, keepdims=True)
    scale = jnp.maximum(scale, TINY)
    mb = (big / scale).astype(BF16)

    def apply(v):
        hi = v.astype(BF16)
        lo = (v - hi.astype(F32)).astype(BF16)
        w = dot(mb, jnp.concatenate([hi, lo], axis=1))
        return w[:, :128] + w[:, 128:]

    v1 = apply(r0)
    v2 = apply(v1)
    v3 = apply(v2)

    def inner(a, b):
        return jnp.sum(a * b, axis=0, keepdims=True)

    tiles[s] = jnp.concatenate(
        [inner(r0, v1), inner(v1, v1), inner(v1, v2), inner(v2, v2), inner(v2, v3), inner(v3, v3),
         jnp.broadcast_to(scale, (1, 128)), jnp.zeros((1, 128), F32)], axis=0)

    def t_copy(k, src):
        return remote(tiles.at[src], tiles.at[src], t_ssem.at[k], t_rsem.at[k], (e, lax.rem(s + k, SHARDS)))

    loop(1, SHARDS, lambda k: t_copy(k, s).start())
    loop(1, SHARDS, lambda k: t_copy(k, lax.rem(s + SHARDS - k, SHARDS)).wait_recv())

    every = tiles[...]
    scales = every[:, 6:7, :]
    top = jnp.max(scales, axis=0, keepdims=True)
    ratio = jnp.broadcast_to(scales / top, every.shape)
    which = lax.broadcasted_iota(jnp.int32, every.shape, 1)
    power = ratio
    weight = jnp.where(which == 0, power, 0.0)
    for k in range(1, 6):
        power = power * ratio
        weight = jnp.where(which == k, power, weight)
    moments = jnp.sum(jnp.sum(every * weight, axis=0), axis=1, keepdims=True)
    m = [None] + [moments[k:k + 1] for k in range(6)]
    top = top[0, :, 0:1]
    coef = step_scalars(m, EPS / top, EPS / top / top)
    rel = scale / top
    coef = [coef[0], coef[1] * rel, coef[2] * rel * rel]
    total = coef[0] * r0 + coef[1] * v1 + coef[2] * v2
    sg[p, c] = (FACTOR / top * total).astype(BF16)

    def s_copy(k, q):
        return remote(sg.at[q, c], sg.at[q, c], s_ssem.at[k], s_rsem.at[k], (e, 2 * chip(k) + c))

    def sf_copy(k, q):
        return remote(sg.at[q, c], sg.at[q, c], sf_ssem.at[k], sf_rsem.at[k], sib)

    def sf_wait(k, q):
        remote(sg.at[q, 1 - c], sg.at[q, 1 - c], sf_ssem.at[k], sf_rsem.at[k], sib).wait_recv()

    loop(1, CHIPS, lambda k: s_copy(k, p).start())
    sf_copy(0, p).start()

    last = r0 - rel * (coef[0] * v1 + coef[1] * v2 + coef[2] * v3)

    def add_av(k, carry):
        q = from_chip(k)
        remote(stage.at[p, 2], av.at[q], av_ssem.at[k], av_rsem.at[k], (e, 2 * q + c)).wait_recv()
        return carry + av[q].astype(F32)

    whole = lax.fori_loop(1, CHIPS, add_av, stage[p, 2].astype(F32))
    fit[...] = (whole - last).astype(BF16)
    returns = []
    for at, d in enumerate(ORDER):
        if d:
            back_copy = remote(fit.at[pl.ds(at * CAP, CAP)], ret.at[pl.ds(d * CAP, CAP)], r_ssem.at[d], r_rsem.at[d], (back(d), s))
            back_copy.start()
            returns.append(back_copy)
        else:
            ret[0:CAP] = fit[at * CAP:(at + 1) * CAP]

    def refit(q, core):
        j = 2 * q + core
        cols = pl.ds(pl.multiple_of(j * 128, 128), 128)
        w = dot(ht[...], sg[q, core]) + down[:, cols].astype(F32)
        w = jnp.concatenate([w[:128] * kb[0, pl.ds(j, 1), :], w[128:] * kb[1, pl.ds(j, 1), :]], axis=0)
        new_ref[0, :, cols] = w.astype(BF16)

    refit(p, c)

    def refit_step(k):
        q = from_chip(k)
        s_copy(k, q).wait_recv()
        sf_copy(k, q).start()
        refit(q, c)
        before = from_chip(k - 1)
        sf_wait(k - 1, before)
        refit(before, 1 - c)

    loop(1, CHIPS, refit_step)
    sf_wait(CHIPS - 1, from_chip(CHIPS - 1))
    refit(from_chip(CHIPS - 1), 1 - c)

    for back_copy in returns:
        back_copy.wait()
    refit_ref[...] = jnp.dot(combining, ret[...].astype(F32), preferred_element_type=F32,
                             precision=lax.Precision.HIGHEST).astype(BF16)

    @pl.when(c == 0)
    def _():
        z_copy(0).wait_send()

    loop(1, 4, lambda i: z_copy(i).wait_send())
    loop(0, CHIPS, lambda q: v_copy(q).wait_send())

    def drain(k):
        ag_copy(k, p).wait_send()
        rs_copy(k, chip(k)).wait_send()
        av_copy(k, chip(k)).wait_send()
        s_copy(k, p).wait_send()

    loop(1, CHIPS, drain)

    def drain_sibling(k):
        fw_copy(k, from_chip(k)).wait_send()
        sf_copy(k, from_chip(k)).wait_send()

    loop(0, CHIPS, drain_sibling)
    loop(1, SHARDS, lambda k: t_copy(k, s).wait_send())


def body(tokens, routes, router_logits, gate_weight, up_weight, down_weight, kept_blocks):
    rows, model = tokens.shape
    width = model // CHIPS
    own = gate_weight.shape[2]
    dma = pltpu.SemaphoreType.DMA
    vmem = pl.BlockSpec(memory_space=pltpu.VMEM)
    anywhere = pl.BlockSpec(memory_space=pl.ANY)
    return pl.pallas_call(
        kernel,
        out_shape=(jax.ShapeDtypeStruct((rows, DW // SHARDS), BF16), jax.ShapeDtypeStruct(down_weight.shape, BF16)),
        in_specs=[anywhere, vmem, vmem, anywhere, anywhere, anywhere, vmem],
        out_specs=(vmem, vmem),
        scratch_shapes=[
            pltpu.VMEM((rows, width), BF16),
            pltpu.VMEM((model, own), BF16),
            pltpu.VMEM((model, own), BF16),
            pltpu.VMEM((own, DW), BF16),
            pltpu.VMEM((ROWS, width), BF16),
            pltpu.VMEM((CHIPS, 2, ROWS // 2, width), BF16),
            pltpu.VMEM((ROWS, own), F32),
            pltpu.VMEM((ROWS, own), F32),
            pltpu.VMEM((ROWS, own), BF16),
            pltpu.VMEM((ROWS, own), BF16),
            pltpu.VMEM((own, ROWS), BF16),
            pltpu.VMEM((CHIPS, own, 128), BF16),
            pltpu.VMEM((2, SHARDS, 128), F32),
            pltpu.VMEM((2, SHARDS, 128), F32),
            pltpu.VMEM((4, 128, 128), F32),
            pltpu.VMEM((CHIPS, 3, 128, 128), BF16),
            pltpu.VMEM((CHIPS, 2, 128, 128), BF16),
            pltpu.VMEM((CHIPS, 128, 128), BF16),
            pltpu.VMEM((SHARDS, 8, 128), F32),
            pltpu.VMEM((CHIPS, 2, 128, 128), BF16),
            pltpu.VMEM((ROWS, 128), BF16),
            pltpu.VMEM((ROWS, 128), BF16),
            dma((4,)),
            dma((4,)), dma((4,)),
            dma((CHIPS,)), dma((CHIPS,)),
            dma((CHIPS,)), dma((CHIPS,)),
            dma((CHIPS,)), dma((CHIPS,)),
            dma((2,)), dma((2,)),
            dma((CHIPS,)), dma((CHIPS,)),
            dma((CHIPS,)), dma((CHIPS,)),
            dma((SHARDS,)), dma((SHARDS,)),
            dma((CHIPS,)), dma((CHIPS,)),
            dma((CHIPS,)), dma((CHIPS,)),
            dma((GROUPS,)), dma((GROUPS,)),
        ],
        compiler_params=pltpu.CompilerParams(collective_id=0, has_side_effects=True, vmem_limit_bytes=48 << 20),
        name="refit",
    )(tokens, routes, router_logits, gate_weight, up_weight, down_weight, kept_blocks)


def solution(mesh):
    in_specs = (
        P("expert", None),
        P("expert", None),
        P("expert", None),
        P("expert", None, "shard"),
        P("expert", None, "shard"),
        P("expert", "shard", None),
        P("expert", "shard", None),
    )
    out_specs = (P("expert", "shard"), P("expert", "shard", None))
    return jax.shard_map(body, mesh=mesh, in_specs=in_specs, out_specs=out_specs, check_vma=False)
```

```python
import functools

import jax
import jax.numpy as jnp
from jax import lax
from jax.experimental import pallas as pl
from jax.experimental.pallas import tpu as pltpu
from jax.sharding import PartitionSpec as P

FF = 8192
DW = 4096
EPS = 1e-6
FACTOR = FF ** -0.5
CAP = 16
GROUPS = 8
CHIPS = 16
SHARDS = 32
ROWS = GROUPS * CAP
PACKED = 96
TINY = 1e-30
MESH = pl.DeviceIdType.MESH
F32 = jnp.float32
BF16 = jnp.bfloat16

ORDER = (1, 3, 5, 7, 0, 2, 4, 6)


def dot(a, b, ca=1, cb=0):
    return lax.dot_general(a, b, (((ca,), (cb,)), ((), ())), preferred_element_type=F32)


def slot_rows(routes, plane):
    rel = [lax.rem(routes[k:k + 1] - plane + GROUPS, GROUPS) for k in range(2)]
    tok = rel[0].shape[1]
    experts = lax.broadcasted_iota(jnp.int32, (GROUPS, tok), 0)
    onehot = [(r == experts).astype(F32) for r in rel]
    earlier = lax.broadcasted_iota(jnp.int32, (tok, tok), 0) < lax.broadcasted_iota(jnp.int32, (tok, tok), 1)
    before = dot((onehot[0] + onehot[1]).astype(BF16), earlier.astype(BF16))
    slots = [jnp.sum(before * o, axis=0, keepdims=True) for o in onehot]
    rows = lax.broadcasted_iota(jnp.int32, (ROWS, tok), 0).astype(F32)
    return [(r * CAP).astype(F32) + s == rows for r, s in zip(rel, slots)]


def packed(m):
    return jnp.concatenate([m[:64], jnp.concatenate([m[64:96, 64:], m[96:, 64:]], axis=1)], axis=0)


def unpacked(m):
    corner = jnp.concatenate([m[64:, :64], m[64:, 64:]], axis=0)
    return jnp.concatenate([m[:64], jnp.concatenate([jnp.transpose(m[:64])[64:], corner], axis=1)], axis=0)


def step_scalars(m, eps1, eps2):
    def form(p, shift):
        total = None
        size = None
        for i, a in enumerate(p):
            for j, b in enumerate(p):
                term = a * b * m[i + j + shift]
                total = term if total is None else total + term
                size = jnp.abs(term) if size is None else size + jnp.abs(term)
        return jnp.maximum(total, 0.0), size

    one = jnp.ones_like(m[1])
    r, s = [one], [one]
    gnorm, _ = form(r, 1)
    out = None
    for it in range(3):
        image, size = form(s, 2)
        image = jnp.maximum(image, 1e-6 * size)
        step = gnorm / (image + eps2)
        term = [step * a for a in s]
        out = term if out is None else [a + b for a, b in zip(out + [0.0] * (len(term) - len(out)), term)]
        if it < 2:
            r = [a - b for a, b in zip(r + [0.0], [0.0] + term)]
            fresh, _ = form(r, 1)
            beta = fresh / (gnorm + eps1)
            s = [a + b for a, b in zip(r, [beta * c for c in s] + [0.0])]
            gnorm = fresh
    return out


def kernel(tok_hbm, routes_hbm, logits_hbm, gate_hbm, up_hbm, down_hbm, kept_hbm,
           sg, ht, refit_ref,
           tok, routes, logits, kept, gate, up, down, outgoing, xg, acc_g, acc_u, hown, hsib, vsib, kb, ksib, gram,
           stage, rs, av, tiles, mine, fit, ret,
           load_sem, z_ssem, z_rsem, ag_ssem, ag_rsem, fw_ssem, fw_rsem, v_ssem, v_rsem, k_sem, h_sem,
           rs_ssem, rs_rsem, av_ssem, av_rsem, t_ssem, t_rsem, s_ssem, s_rsem, sf_ssem, sf_rsem, r_ssem, r_rsem, own_sem):
    e = lax.axis_index("expert")
    s = lax.axis_index("shard")
    p = s // 2
    c = lax.rem(s, 2)
    sib = (e, 2 * p + 1 - c)
    width = tok.shape[1]

    def offset(k):
        j = lax.rem(7 * k, CHIPS)
        return j // 4, lax.rem(j, 4)

    def chip(k):
        dy, dx = offset(k)
        return 4 * lax.rem(p // 4 + dy, 4) + lax.rem(lax.rem(p, 4) + dx, 4)

    def from_chip(k):
        dy, dx = offset(k)
        return 4 * lax.rem(p // 4 + 4 - dy, 4) + lax.rem(lax.rem(p, 4) + 4 - dx, 4)

    def plane(d):
        return lax.rem(e + d, GROUPS)

    def back(d):
        return lax.rem(e + GROUPS - d, GROUPS)

    def remote(src, dst, ssem, rsem, device):
        return pltpu.make_async_remote_copy(src_ref=src, dst_ref=dst, send_sem=ssem, recv_sem=rsem,
                                            device_id=device, device_id_type=MESH)

    def loop(lo, hi, f):
        lax.fori_loop(lo, hi, lambda k, _: (f(k), 0)[1], 0)

    pending = {}

    def finish():
        for name in list(pending):
            pending.pop(name)()

    barrier = pltpu.get_barrier_semaphore()
    loop(1, GROUPS, lambda d: pl.semaphore_signal(barrier, inc=1, device_id=(plane(d), s), device_id_type=MESH))
    loop(1, SHARDS, lambda k: pl.semaphore_signal(barrier, inc=1, device_id=(e, lax.rem(s + k, SHARDS)), device_id_type=MESH))

    loads = [
        pltpu.make_async_copy(tok_hbm.at[:, pl.ds(pl.multiple_of(p * width, 128), width)], tok, load_sem.at[0]),
        pltpu.make_async_copy(routes_hbm, routes, load_sem.at[1]),
        pltpu.make_async_copy(logits_hbm, logits, load_sem.at[2]),
        pltpu.make_async_copy(kept_hbm, kept, load_sem.at[3]),
        pltpu.make_async_copy(gate_hbm.at[0], gate, load_sem.at[4]),
        pltpu.make_async_copy(up_hbm.at[0], up, load_sem.at[5]),
        pltpu.make_async_copy(down_hbm.at[0], down, load_sem.at[6]),
    ]
    for load in loads:
        load.start()

    for load in loads[:4]:
        load.wait()
    match = slot_rows(routes[...], e)
    placing = (match[0] | match[1]).astype(BF16)
    outgoing[...] = dot(placing, tok[...]).astype(BF16)
    logit = logits[0:1] - logits[1:2]
    share = 1.0 / (1.0 + jnp.exp(-logit))
    combining = jnp.where(match[0], share, 0.0) + jnp.where(match[1], 1.0 - share, 0.0)
    row = lax.broadcasted_iota(jnp.int32, (2, 128), 0)
    for f in range(2):
        kb[f] = dot(kept[0].astype(F32), (row == f).astype(F32), 0, 0)

    pending["loads"] = lambda: [load.wait() for load in loads[4:]]
    pl.semaphore_wait(barrier, GROUPS - 1 + SHARDS - 1)

    def z_copy(i):
        d = 2 * i + 1 - c
        return remote(outgoing.at[pl.ds(pl.multiple_of(d * CAP, CAP), CAP)],
                      xg.at[p, c, pl.ds(pl.multiple_of(i * CAP, CAP), CAP)],
                      z_ssem.at[i], z_rsem.at[i], (plane(d), s))

    @pl.when(c == 0)
    def _():
        z_copy(0).start()

    @pl.when(c == 1)
    def _():
        xg[p, 1, 0:CAP] = outgoing[0:CAP]

    loop(1, 4, lambda i: z_copy(i).start())

    def z_sent():
        @pl.when(c == 0)
        def _():
            z_copy(0).wait_send()

        loop(1, 4, lambda i: z_copy(i).wait_send())

    def z_arrived():
        @pl.when(c == 0)
        def _():
            z_copy(0).wait_recv()

        loop(1, 4, lambda i: z_copy(i).wait_recv())

    pending["z"] = z_sent

    def v_copy(q):
        return remote(down_hbm.at[0, :, pl.ds(pl.multiple_of((2 * q + 1 - c) * 128, 128), 128)], vsib.at[q],
                      v_ssem.at[q], v_rsem.at[q], sib)

    loop(0, CHIPS, lambda q: v_copy(q).start())
    k_copy = remote(kb, ksib, k_sem.at[0], k_sem.at[1], sib)
    k_copy.start()
    pending["v"] = lambda: loop(0, CHIPS, lambda q: v_copy(q).wait())
    pending["k"] = k_copy.wait
    z_arrived()

    def ag_copy(k, q):
        return remote(xg.at[q, c], xg.at[q, c], ag_ssem.at[k], ag_rsem.at[k], (e, 2 * chip(k) + c))

    def fw_copy(k, q):
        return remote(xg.at[q, c], xg.at[q, c], fw_ssem.at[k], fw_rsem.at[k], sib)

    def fw_wait(k, q):
        remote(xg.at[q, 1 - c], xg.at[q, 1 - c], fw_ssem.at[k], fw_rsem.at[k], sib).wait_recv()

    loop(1, CHIPS, lambda k: ag_copy(k, p).start())
    fw_copy(0, p).start()
    pending["ag"] = lambda: loop(1, CHIPS, lambda k: ag_copy(k, p).wait_send())
    pending["fw"] = lambda: loop(0, CHIPS, lambda k: fw_copy(k, from_chip(k)).wait_send())
    pending.pop("loads")()
    acc_g[...] = jnp.zeros_like(acc_g)
    acc_u[...] = jnp.zeros_like(acc_u)

    def expand(k):
        q = from_chip(k)
        fw_wait(k, q)
        x = xg[q].reshape(ROWS, width)
        rows = pl.ds(pl.multiple_of(q * width, 128), width)
        acc_g[...] += dot(x, gate[rows, :])
        acc_u[...] += dot(x, up[rows, :])

    def gather_step(k):
        q = from_chip(k)
        ag_copy(k, q).wait_recv()
        fw_copy(k, q).start()
        expand(k - 1)

    loop(1, CHIPS, gather_step)
    expand(CHIPS - 1)
    g = acc_g[...]
    h32 = g / (1.0 + jnp.exp(-g)) * acc_u[...]
    hown[...] = h32.astype(BF16)
    h_copy = remote(hown, hsib, h_sem.at[0], h_sem.at[1], sib)
    h_copy.start()
    ht[...] = jnp.transpose(hown[...].astype(F32)).astype(BF16)

    def grams(h, base):
        for f in range(2):
            hf = h[:, f * 128:(f + 1) * 128]
            gram[base + f] = packed(FACTOR * FACTOR * dot(hf, hf, 1, 1))

    grams(hown[...], 0)
    pending.pop("v")()
    pending.pop("k")()
    h_copy.wait()
    grams(hsib[...], 2)

    def masked(v, k0, k1):
        return jnp.concatenate([v[:128] * (1.0 - k0).astype(BF16), v[128:] * (1.0 - k1).astype(BF16)], axis=0)

    def rs_copy(k, q):
        return remote(stage.at[q, pl.ds(0, PACKED + 128)], rs.at[p], rs_ssem.at[k], rs_rsem.at[k], (e, 2 * q + c))

    def av_copy(k, q):
        return remote(stage.at[q, pl.ds(PACKED + 128, 128)], av.at[p], av_ssem.at[k], av_rsem.at[k], (e, 2 * q + c))

    def partial(q):
        j = 2 * q + c
        ko = [kb[f, pl.ds(j, 1), :] for f in range(2)]
        ks = [ksib[f, pl.ds(j, 1), :] for f in range(2)]
        stage[q, 0:PACKED] = (ko[0] * gram[0] + ko[1] * gram[1] + ks[0] * gram[2] + ks[1] * gram[3]).astype(BF16)
        vo = down[:, pl.ds(pl.multiple_of(j * 128, 128), 128)]
        vs = vsib[q]
        both = dot(hown[...], jnp.concatenate([masked(vo, *ko), vo], axis=1))
        both += dot(hsib[...], jnp.concatenate([masked(vs, *ks), vs], axis=1))
        both = (FACTOR * both).astype(BF16)
        stage[q, PACKED:PACKED + 128] = both[:, :128]
        stage[q, PACKED + 128:] = both[:, 128:]

    def send_partial(k):
        q = chip(k)
        partial(q)
        rs_copy(k, q).start()

    loop(1, CHIPS, send_partial)
    pending["rs"] = lambda: loop(1, CHIPS, lambda k: rs_copy(k, chip(k)).wait_send())
    partial(p)

    def rs_in(k, q):
        return remote(stage.at[p, pl.ds(0, PACKED + 128)], rs.at[q], rs_ssem.at[k], rs_rsem.at[k], (e, 2 * q + c))

    def av_in(k, q):
        return remote(stage.at[p, pl.ds(PACKED + 128, 128)], av.at[q], av_ssem.at[k], av_rsem.at[k], (e, 2 * q + c))


    def add_up(k, carry):
        q = from_chip(k)
        rs_in(k, q).wait_recv()
        return carry + rs[q].astype(F32)

    summed = lax.fori_loop(1, CHIPS, add_up, stage[p, 0:PACKED + 128].astype(F32))
    big, r0 = unpacked(summed[:PACKED]), summed[PACKED:]

    eye = lax.broadcasted_iota(jnp.int32, (128, 128), 0) == lax.broadcasted_iota(jnp.int32, (128, 128), 1)
    scale = jnp.sum(jnp.sum(jnp.where(eye, big, 0.0), axis=0, keepdims=True), axis=1, keepdims=True)
    scale = jnp.maximum(scale, TINY)
    mb = (big / scale).astype(BF16)

    def apply(v):
        hi = v.astype(BF16)
        lo = (v - hi.astype(F32)).astype(BF16)
        w = dot(mb, jnp.concatenate([hi, lo], axis=1))
        return w[:, :128] + w[:, 128:]

    v1 = apply(r0)
    v2 = apply(v1)
    v3 = apply(v2)

    def inner(a, b):
        return jnp.sum(a * b, axis=0, keepdims=True)

    tiles[s] = jnp.concatenate(
        [inner(r0, v1), inner(v1, v1), inner(v1, v2), inner(v2, v2), inner(v2, v3), inner(v3, v3),
         jnp.broadcast_to(scale, (1, 128)), jnp.zeros((1, 128), F32)], axis=0)

    def t_copy(k, src):
        return remote(tiles.at[src], tiles.at[src], t_ssem.at[k], t_rsem.at[k], (e, lax.rem(s + k, SHARDS)))

    loop(1, SHARDS, lambda k: t_copy(k, s).start())
    loop(1, CHIPS, lambda k: av_copy(k, chip(k)).start())
    pending["av"] = lambda: loop(1, CHIPS, lambda k: av_copy(k, chip(k)).wait_send())
    pending["av in"] = lambda: loop(1, CHIPS, lambda k: av_in(k, from_chip(k)).wait_recv())
    pending["t"] = lambda: loop(1, SHARDS, lambda k: t_copy(k, s).wait_send())
    loop(1, SHARDS, lambda k: t_copy(k, lax.rem(s + SHARDS - k, SHARDS)).wait_recv())

    every = tiles[...]
    scales = every[:, 6:7, :]
    top = jnp.max(scales, axis=0, keepdims=True)
    ratio = jnp.broadcast_to(scales / top, every.shape)
    which = lax.broadcasted_iota(jnp.int32, every.shape, 1)
    power = ratio
    weight = jnp.where(which == 0, power, 0.0)
    for k in range(1, 6):
        power = power * ratio
        weight = jnp.where(which == k, power, weight)
    moments = jnp.sum(jnp.sum(every * weight, axis=0), axis=1, keepdims=True)
    m = [None] + [moments[k:k + 1] for k in range(6)]
    top = top[0, :, 0:1]
    coef = step_scalars(m, EPS / top, EPS / top / top)
    rel = scale / top
    coef = [coef[0], coef[1] * rel, coef[2] * rel * rel]
    total = coef[0] * r0 + coef[1] * v1 + coef[2] * v2
    mine[...] = (FACTOR / top * total).astype(BF16)

    own_copy = pltpu.make_async_copy(mine, sg.at[p, c], own_sem)
    own_copy.start()

    def s_copy(k):
        return remote(mine, sg.at[p, c], s_ssem.at[k], s_rsem.at[k], (e, 2 * chip(k) + c))

    def s_in(k, q):
        return remote(mine, sg.at[q, c], s_ssem.at[k], s_rsem.at[k], (e, 2 * chip(k) + c))

    def sf_copy(k, q):
        return remote(sg.at[q, c], sg.at[q, c], sf_ssem.at[k], sf_rsem.at[k], sib)

    def sf_wait(k, q):
        remote(sg.at[q, 1 - c], sg.at[q, 1 - c], sf_ssem.at[k], sf_rsem.at[k], sib).wait_recv()

    own_share = remote(mine, sg.at[p, c], sf_ssem.at[0], sf_rsem.at[0], sib)
    own_share.start()
    loop(1, CHIPS, lambda k: s_copy(k).start())
    pending["s"] = lambda: loop(1, CHIPS, lambda k: s_copy(k).wait_send())
    pending["sf"] = lambda: (own_share.wait_send(), loop(1, CHIPS, lambda k: sf_copy(k, from_chip(k)).wait_send()))
    pending["own"] = own_copy.wait

    last = r0 - rel * (coef[0] * v1 + coef[1] * v2 + coef[2] * v3)

    def add_av(k, carry):
        q = from_chip(k)
        av_in(k, q).wait_recv()
        return carry + av[q].astype(F32)

    pending.pop("av in")
    whole = lax.fori_loop(1, CHIPS, add_av, stage[p, PACKED + 128:].astype(F32))
    fit[...] = (whole - last).astype(BF16)
    returns = []
    for at, d in enumerate(ORDER):
        if d:
            back_copy = remote(fit.at[pl.ds(at * CAP, CAP)], ret.at[pl.ds(d * CAP, CAP)], r_ssem.at[d], r_rsem.at[d], (back(d), s))
            back_copy.start()
            returns.append(back_copy)
        else:
            ret[0:CAP] = fit[at * CAP:(at + 1) * CAP]

    def share_step(k):
        q = from_chip(k)
        s_in(k, q).wait_recv()
        sf_copy(k, q).start()

    loop(1, CHIPS, share_step)

    for back_copy in returns:
        back_copy.wait()
    refit_ref[...] = lax.dot_general(combining, ret[...].astype(F32), (((0,), (0,)), ((), ())),
                                     precision=lax.Precision.HIGHEST, preferred_element_type=F32).astype(BF16)
    loop(0, CHIPS, lambda k: sf_wait(k, from_chip(k)))
    finish()


PIECES = 4


def apply_kernel(sg_hbm, ht_hbm, refit_hbm, down_hbm, kept_hbm, refit_ref, new_hbm, sg, ht, down, kept, new, sem, out_sem):
    wide = DW // PIECES
    chips = CHIPS // PIECES

    def cols(i):
        return pl.ds(i * wide, wide)

    small = [pltpu.make_async_copy(a, b, sem.at[i]) for i, (a, b) in enumerate([(ht_hbm, ht), (kept_hbm, kept), (refit_hbm, refit_ref)])]
    parts = []
    for i in range(PIECES):
        parts.append((
            pltpu.make_async_copy(sg_hbm.at[pl.ds(i * chips, chips)], sg.at[pl.ds(i * chips, chips)], sem.at[3 + 2 * i]),
            pltpu.make_async_copy(down_hbm.at[0, :, cols(i)], down.at[:, cols(i)], sem.at[4 + 2 * i])))
    for copy in small[:2] + [copy for part in parts for copy in part] + small[2:]:
        copy.start()
    small[0].wait()
    small[1].wait()
    h = ht[...]
    row = lax.broadcasted_iota(jnp.int32, (2, 128), 0)
    keeps = [dot(kept[0].astype(F32), (row == f).astype(F32), 0, 0) for f in range(2)]
    writes = []
    for i in range(PIECES):
        for copy in parts[i]:
            copy.wait()
        for n in range(2 * chips):
            j = 2 * chips * i + n
            at = slice(j * 128, (j + 1) * 128)
            w = dot(h, sg[j // 2, j % 2]) + down[:, at].astype(F32)
            new[:128, at] = (w[:128] * keeps[0][j:j + 1]).astype(BF16)
            new[128:, at] = (w[128:] * keeps[1][j:j + 1]).astype(BF16)
        write = pltpu.make_async_copy(new.at[:, cols(i)], new_hbm.at[0, :, cols(i)], out_sem.at[i])
        write.start()
        writes.append(write)
    for copy in writes + small[2:]:
        copy.wait()


def body(tokens, routes, router_logits, gate_weight, up_weight, down_weight, kept_blocks):
    rows, model = tokens.shape
    width = model // CHIPS
    own = gate_weight.shape[2]
    dma = pltpu.SemaphoreType.DMA
    vmem = pl.BlockSpec(memory_space=pltpu.VMEM)
    hbm = pl.BlockSpec(memory_space=pltpu.HBM)
    gathered, turned, refit = pl.pallas_call(
        kernel,
        out_shape=(jax.ShapeDtypeStruct((CHIPS, 2, 128, 128), BF16), jax.ShapeDtypeStruct((own, ROWS), BF16),
                   jax.ShapeDtypeStruct((rows, DW // SHARDS), BF16)),
        in_specs=[hbm] * 7,
        out_specs=(hbm, vmem, vmem),
        scratch_shapes=[
            pltpu.VMEM((rows, width), BF16),
            pltpu.VMEM((2, rows), jnp.int32),
            pltpu.VMEM((2, rows), F32),
            pltpu.VMEM(kept_blocks.shape, jnp.int32),
            pltpu.VMEM((model, own), BF16),
            pltpu.VMEM((model, own), BF16),
            pltpu.VMEM((own, DW), BF16),
            pltpu.VMEM((ROWS, width), BF16),
            pltpu.VMEM((CHIPS, 2, ROWS // 2, width), BF16),
            pltpu.VMEM((ROWS, own), F32),
            pltpu.VMEM((ROWS, own), F32),
            pltpu.VMEM((ROWS, own), BF16),
            pltpu.VMEM((ROWS, own), BF16),
            pltpu.VMEM((CHIPS, own, 128), BF16),
            pltpu.VMEM((2, SHARDS, 128), F32),
            pltpu.VMEM((2, SHARDS, 128), F32),
            pltpu.VMEM((4, PACKED, 128), F32),
            pltpu.VMEM((CHIPS, PACKED + 256, 128), BF16),
            pltpu.VMEM((CHIPS, PACKED + 128, 128), BF16),
            pltpu.VMEM((CHIPS, 128, 128), BF16),
            pltpu.VMEM((SHARDS, 8, 128), F32),
            pltpu.VMEM((ROWS, 128), BF16),
            pltpu.VMEM((ROWS, 128), BF16),
            pltpu.VMEM((ROWS, 128), BF16),
            dma((7,)),
            dma((4,)), dma((4,)),
            dma((CHIPS,)), dma((CHIPS,)),
            dma((CHIPS,)), dma((CHIPS,)),
            dma((CHIPS,)), dma((CHIPS,)),
            dma((2,)), dma((2,)),
            dma((CHIPS,)), dma((CHIPS,)),
            dma((CHIPS,)), dma((CHIPS,)),
            dma((SHARDS,)), dma((SHARDS,)),
            dma((CHIPS,)), dma((CHIPS,)),
            dma((CHIPS,)), dma((CHIPS,)),
            dma((GROUPS,)), dma((GROUPS,)),
            dma,
        ],
        compiler_params=pltpu.CompilerParams(collective_id=0, has_side_effects=True, vmem_limit_bytes=60 << 20),
        name="refit",
    )(tokens, routes.T, router_logits.T, gate_weight, up_weight, down_weight, kept_blocks)
    return pl.pallas_call(
        apply_kernel,
        out_shape=(jax.ShapeDtypeStruct(refit.shape, BF16), jax.ShapeDtypeStruct(down_weight.shape, BF16)),
        in_specs=[hbm] * 5,
        out_specs=(vmem, hbm),
        scratch_shapes=[
            pltpu.VMEM(gathered.shape, BF16),
            pltpu.VMEM(turned.shape, BF16),
            pltpu.VMEM((own, DW), BF16),
            pltpu.VMEM(kept_blocks.shape, jnp.int32),
            pltpu.VMEM((own, DW), BF16),
            dma((3 + 2 * PIECES,)),
            dma((PIECES,)),
        ],
        compiler_params=pltpu.CompilerParams(vmem_limit_bytes=60 << 20),
        name="apply",
    )(gathered, turned, refit, down_weight, kept_blocks)


def solution(mesh):
    in_specs = (
        P("expert", None),
        P("expert", None),
        P("expert", None),
        P("expert", None, "shard"),
        P("expert", None, "shard"),
        P("expert", "shard", None),
        P("expert", "shard", None),
    )
    out_specs = (P("expert", "shard"), P("expert", "shard", None))
    return jax.shard_map(body, mesh=mesh, in_specs=in_specs, out_specs=out_specs, check_vma=False)
```

```python
import functools

import jax
import jax.numpy as jnp
from jax import lax
from jax.experimental import pallas as pl
from jax.experimental.pallas import tpu as pltpu
from jax.sharding import PartitionSpec as P

FF = 8192
DW = 4096
EPS = 1e-6
FACTOR = FF ** -0.5
CAP = 16
GROUPS = 8
CHIPS = 16
SHARDS = 32
ROWS = GROUPS * CAP
PACKED = 96
TINY = 1e-30
MESH = pl.DeviceIdType.MESH
F32 = jnp.float32
BF16 = jnp.bfloat16

ORDER = (1, 3, 5, 7, 0, 2, 4, 6)


def dot(a, b, ca=1, cb=0):
    return lax.dot_general(a, b, (((ca,), (cb,)), ((), ())), preferred_element_type=F32)


def slot_rows(routes, plane):
    rel = [lax.rem(routes[k:k + 1] - plane + GROUPS, GROUPS) for k in range(2)]
    tok = rel[0].shape[1]
    experts = lax.broadcasted_iota(jnp.int32, (GROUPS, tok), 0)
    onehot = [(r == experts).astype(F32) for r in rel]
    earlier = lax.broadcasted_iota(jnp.int32, (tok, tok), 0) < lax.broadcasted_iota(jnp.int32, (tok, tok), 1)
    before = dot((onehot[0] + onehot[1]).astype(BF16), earlier.astype(BF16))
    slots = [jnp.sum(before * o, axis=0, keepdims=True) for o in onehot]
    rows = lax.broadcasted_iota(jnp.int32, (ROWS, tok), 0).astype(F32)
    return [(r * CAP).astype(F32) + s == rows for r, s in zip(rel, slots)]


def packed(m):
    return jnp.concatenate([m[:64], jnp.concatenate([m[64:96, 64:], m[96:, 64:]], axis=1)], axis=0)


def unpacked(m):
    corner = jnp.concatenate([m[64:, :64], m[64:, 64:]], axis=0)
    return jnp.concatenate([m[:64], jnp.concatenate([jnp.transpose(m[:64])[64:], corner], axis=1)], axis=0)


def step_scalars(m, eps1, eps2):
    def form(p, shift):
        total = None
        size = None
        for i, a in enumerate(p):
            for j, b in enumerate(p):
                term = a * b * m[i + j + shift]
                total = term if total is None else total + term
                size = jnp.abs(term) if size is None else size + jnp.abs(term)
        return jnp.maximum(total, 0.0), size

    one = jnp.ones_like(m[1])
    r, s = [one], [one]
    gnorm, _ = form(r, 1)
    out = None
    for it in range(3):
        image, size = form(s, 2)
        image = jnp.maximum(image, 1e-6 * size)
        step = gnorm / (image + eps2)
        term = [step * a for a in s]
        out = term if out is None else [a + b for a, b in zip(out + [0.0] * (len(term) - len(out)), term)]
        if it < 2:
            r = [a - b for a, b in zip(r + [0.0], [0.0] + term)]
            fresh, _ = form(r, 1)
            beta = fresh / (gnorm + eps1)
            s = [a + b for a, b in zip(r, [beta * c for c in s] + [0.0])]
            gnorm = fresh
    return out


def kernel(tok_hbm, routes_hbm, logits_hbm, gate_hbm, up_hbm, down_hbm, kept_hbm,
           sg, ht, refit_ref,
           tok, tokd, routes, logits, kept, gate, up, down, outgoing, outd, xg, xd, acc_g, acc_u, hown, hsib, vsib, kb, ksib, gram,
           stage, rs, av, tiles, mine, fit, ret,
           load_sem, z_ssem, z_rsem, d_ssem, d_rsem, df_ssem, df_rsem, ag_ssem, ag_rsem, fw_ssem, fw_rsem, v_ssem, v_rsem, k_sem, h_sem,
           rs_ssem, rs_rsem, av_ssem, av_rsem, t_ssem, t_rsem, s_ssem, s_rsem, sf_ssem, sf_rsem, r_ssem, r_rsem, own_sem):
    e = lax.axis_index("expert")
    s = lax.axis_index("shard")
    p = s // 2
    c = lax.rem(s, 2)
    sib = (e, 2 * p + 1 - c)
    width = tok.shape[1]
    direct = tokd.shape[1]
    planar = CHIPS * width

    def offset(k):
        j = lax.rem(7 * k, CHIPS)
        return j // 4, lax.rem(j, 4)

    def chip(k):
        dy, dx = offset(k)
        return 4 * lax.rem(p // 4 + dy, 4) + lax.rem(lax.rem(p, 4) + dx, 4)

    def from_chip(k):
        dy, dx = offset(k)
        return 4 * lax.rem(p // 4 + 4 - dy, 4) + lax.rem(lax.rem(p, 4) + 4 - dx, 4)

    def plane(d):
        return lax.rem(e + d, GROUPS)

    def back(d):
        return lax.rem(e + GROUPS - d, GROUPS)

    def remote(src, dst, ssem, rsem, device):
        return pltpu.make_async_remote_copy(src_ref=src, dst_ref=dst, send_sem=ssem, recv_sem=rsem,
                                            device_id=device, device_id_type=MESH)

    def loop(lo, hi, f):
        lax.fori_loop(lo, hi, lambda k, _: (f(k), 0)[1], 0)

    pending = {}

    def finish():
        for name in list(pending):
            pending.pop(name)()

    barrier = pltpu.get_barrier_semaphore()
    loop(1, GROUPS, lambda d: pl.semaphore_signal(barrier, inc=1, device_id=(plane(d), s), device_id_type=MESH))
    loop(1, SHARDS, lambda k: pl.semaphore_signal(barrier, inc=1, device_id=(e, lax.rem(s + k, SHARDS)), device_id_type=MESH))

    loads = [
        pltpu.make_async_copy(tok_hbm.at[:, pl.ds(pl.multiple_of(p * width, 128), width)], tok, load_sem.at[0]),
        pltpu.make_async_copy(routes_hbm, routes, load_sem.at[1]),
        pltpu.make_async_copy(logits_hbm, logits, load_sem.at[2]),
        pltpu.make_async_copy(kept_hbm, kept, load_sem.at[3]),
        pltpu.make_async_copy(gate_hbm.at[0], gate, load_sem.at[4]),
        pltpu.make_async_copy(up_hbm.at[0], up, load_sem.at[5]),
        pltpu.make_async_copy(down_hbm.at[0], down, load_sem.at[6]),
        pltpu.make_async_copy(tok_hbm.at[:, pl.ds(planar, direct)], tokd, load_sem.at[7]),
    ]
    for load in [loads[0], loads[7]] + loads[1:7]:
        load.start()

    for load in loads[:4]:
        load.wait()
    match = slot_rows(routes[...], e)
    placing = (match[0] | match[1]).astype(BF16)
    outgoing[...] = dot(placing, tok[...]).astype(BF16)
    loads[7].wait()
    outd[...] = dot(placing, tokd[...]).astype(BF16)
    logit = logits[0:1] - logits[1:2]
    share = 1.0 / (1.0 + jnp.exp(-logit))
    combining = jnp.where(match[0], share, 0.0) + jnp.where(match[1], 1.0 - share, 0.0)
    row = lax.broadcasted_iota(jnp.int32, (2, 128), 0)
    for f in range(2):
        kb[f] = dot(kept[0].astype(F32), (row == f).astype(F32), 0, 0)

    pending["loads"] = lambda: [load.wait() for load in loads[4:7]]
    pl.semaphore_wait(barrier, GROUPS - 1 + SHARDS - 1)

    def slots(i):
        return pl.ds(pl.multiple_of(i * CAP, CAP), CAP)

    def z_copy(i):
        d = 2 * i + 1 - c
        return remote(outgoing.at[slots(d)], xg.at[p, c, slots(i)], z_ssem.at[i], z_rsem.at[i], (plane(d), s))

    def d_copy(i):
        d = 2 * i + 1 - c
        return remote(outd.at[slots(d)], xd.at[c, slots(i)], d_ssem.at[i], d_rsem.at[i], (plane(d), s))

    @pl.when(c == 0)
    def _():
        z_copy(0).start()

    loop(1, 4, lambda i: z_copy(i).start())

    @pl.when(c == 0)
    def _():
        d_copy(0).start()

    loop(1, 4, lambda i: d_copy(i).start())

    @pl.when(c == 1)
    def _():
        xg[p, 1, 0:CAP] = outgoing[0:CAP]
        xd[1, 0:CAP] = outd[0:CAP]

    def z_sent():
        @pl.when(c == 0)
        def _():
            z_copy(0).wait_send()
            d_copy(0).wait_send()

        loop(1, 4, lambda i: z_copy(i).wait_send())
        loop(1, 4, lambda i: d_copy(i).wait_send())

    def z_arrived():
        @pl.when(c == 0)
        def _():
            z_copy(0).wait_recv()

        loop(1, 4, lambda i: z_copy(i).wait_recv())

    pending["z"] = z_sent

    def v_copy(q):
        return remote(down_hbm.at[0, :, pl.ds(pl.multiple_of((2 * q + 1 - c) * 128, 128), 128)], vsib.at[q],
                      v_ssem.at[q], v_rsem.at[q], sib)

    loop(0, CHIPS, lambda q: v_copy(q).start())
    k_copy = remote(kb, ksib, k_sem.at[0], k_sem.at[1], sib)
    k_copy.start()
    pending["v"] = lambda: loop(0, CHIPS, lambda q: v_copy(q).wait())
    pending["k"] = k_copy.wait
    z_arrived()

    def ag_copy(k, q):
        return remote(xg.at[q, c], xg.at[q, c], ag_ssem.at[k], ag_rsem.at[k], (e, 2 * chip(k) + c))

    def fw_copy(k, q):
        return remote(xg.at[q, c], xg.at[q, c], fw_ssem.at[k], fw_rsem.at[k], sib)

    def fw_wait(k, q):
        remote(xg.at[q, 1 - c], xg.at[q, 1 - c], fw_ssem.at[k], fw_rsem.at[k], sib).wait_recv()

    loop(1, CHIPS, lambda k: ag_copy(k, p).start())
    fw_copy(0, p).start()
    pending["ag"] = lambda: loop(1, CHIPS, lambda k: ag_copy(k, p).wait_send())

    def df_copy(i):
        return remote(xd.at[c, slots(i)], xd.at[c, slots(i)], df_ssem.at[i], df_rsem.at[i], sib)

    def df_wait(i):
        remote(xd.at[1 - c, slots(i)], xd.at[1 - c, slots(i)], df_ssem.at[i], df_rsem.at[i], sib).wait_recv()

    @pl.when(c == 0)
    def _():
        d_copy(0).wait_recv()

    df_copy(0).start()

    def direct_step(i):
        d_copy(i).wait_recv()
        df_copy(i).start()

    loop(1, 4, direct_step)
    pending["df"] = lambda: loop(0, 4, lambda i: df_copy(i).wait_send())
    pending["fw"] = lambda: loop(0, CHIPS, lambda k: fw_copy(k, from_chip(k)).wait_send())
    pending.pop("loads")()
    acc_g[...] = jnp.zeros_like(acc_g)
    acc_u[...] = jnp.zeros_like(acc_u)

    def expand(k):
        q = from_chip(k)
        fw_wait(k, q)
        x = xg[q].reshape(ROWS, width)
        rows = pl.ds(pl.multiple_of(q * width, 128), width)
        acc_g[...] += dot(x, gate[rows, :])
        acc_u[...] += dot(x, up[rows, :])

    def expand_direct(n):
        x = xd[:, :, pl.ds(pl.multiple_of(n * width, 128), width)].reshape(ROWS, width)
        rows = pl.ds(pl.multiple_of(planar + n * width, 128), width)
        acc_g[...] += dot(x, gate[rows, :])
        acc_u[...] += dot(x, up[rows, :])

    def gather_step(k):
        q = from_chip(k)
        ag_copy(k, q).wait_recv()
        fw_copy(k, q).start()

    half = direct // width
    gather_step(1)
    loop(0, 4, df_wait)
    expand_direct(0)

    def early(k):
        gather_step(k)
        expand_direct(k - 1)

    def late(k):
        gather_step(k)
        expand(2 * (k - half - 1))
        expand(2 * (k - half - 1) + 1)

    loop(2, half + 1, early)
    loop(half + 1, CHIPS, late)
    loop(2 * (CHIPS - half - 1), CHIPS, expand)
    g = acc_g[...]
    h32 = g / (1.0 + jnp.exp(-g)) * acc_u[...]
    hown[...] = h32.astype(BF16)
    h_copy = remote(hown, hsib, h_sem.at[0], h_sem.at[1], sib)
    h_copy.start()
    ht[...] = jnp.transpose(hown[...].astype(F32)).astype(BF16)

    def grams(h, base):
        for f in range(2):
            hf = h[:, f * 128:(f + 1) * 128]
            gram[base + f] = packed(FACTOR * FACTOR * dot(hf, hf, 1, 1))

    grams(hown[...], 0)
    pending.pop("v")()
    pending.pop("k")()
    h_copy.wait()
    grams(hsib[...], 2)

    def masked(v, k0, k1):
        return jnp.concatenate([v[:128] * (1.0 - k0).astype(BF16), v[128:] * (1.0 - k1).astype(BF16)], axis=0)

    def rs_copy(k, q):
        return remote(stage.at[q, pl.ds(0, PACKED + 128)], rs.at[p], rs_ssem.at[k], rs_rsem.at[k], (e, 2 * q + c))

    def av_copy(k, q):
        return remote(stage.at[q, pl.ds(PACKED + 128, 128)], av.at[p], av_ssem.at[k], av_rsem.at[k], (e, 2 * q + c))

    def partial(q):
        j = 2 * q + c
        ko = [kb[f, pl.ds(j, 1), :] for f in range(2)]
        ks = [ksib[f, pl.ds(j, 1), :] for f in range(2)]
        stage[q, 0:PACKED] = (ko[0] * gram[0] + ko[1] * gram[1] + ks[0] * gram[2] + ks[1] * gram[3]).astype(BF16)
        vo = down[:, pl.ds(pl.multiple_of(j * 128, 128), 128)]
        vs = vsib[q]
        both = dot(hown[...], jnp.concatenate([masked(vo, *ko), vo], axis=1))
        both += dot(hsib[...], jnp.concatenate([masked(vs, *ks), vs], axis=1))
        both = (FACTOR * both).astype(BF16)
        stage[q, PACKED:PACKED + 128] = both[:, :128]
        stage[q, PACKED + 128:] = both[:, 128:]

    def send_partial(k):
        q = chip(k)
        partial(q)
        rs_copy(k, q).start()

    loop(1, CHIPS, send_partial)
    pending["rs"] = lambda: loop(1, CHIPS, lambda k: rs_copy(k, chip(k)).wait_send())
    partial(p)

    def rs_in(k, q):
        return remote(stage.at[p, pl.ds(0, PACKED + 128)], rs.at[q], rs_ssem.at[k], rs_rsem.at[k], (e, 2 * q + c))

    def av_in(k, q):
        return remote(stage.at[p, pl.ds(PACKED + 128, 128)], av.at[q], av_ssem.at[k], av_rsem.at[k], (e, 2 * q + c))


    def add_up(k, carry):
        q = from_chip(k)
        rs_in(k, q).wait_recv()
        return carry + rs[q].astype(F32)

    summed = lax.fori_loop(1, CHIPS, add_up, stage[p, 0:PACKED + 128].astype(F32))
    big, r0 = unpacked(summed[:PACKED]), summed[PACKED:]

    eye = lax.broadcasted_iota(jnp.int32, (128, 128), 0) == lax.broadcasted_iota(jnp.int32, (128, 128), 1)
    scale = jnp.sum(jnp.sum(jnp.where(eye, big, 0.0), axis=0, keepdims=True), axis=1, keepdims=True)
    scale = jnp.maximum(scale, TINY)
    mb = (big / scale).astype(BF16)

    def apply(v):
        hi = v.astype(BF16)
        lo = (v - hi.astype(F32)).astype(BF16)
        w = dot(mb, jnp.concatenate([hi, lo], axis=1))
        return w[:, :128] + w[:, 128:]

    v1 = apply(r0)
    v2 = apply(v1)
    v3 = apply(v2)

    def inner(a, b):
        return jnp.sum(a * b, axis=0, keepdims=True)

    tiles[s] = jnp.concatenate(
        [inner(r0, v1), inner(v1, v1), inner(v1, v2), inner(v2, v2), inner(v2, v3), inner(v3, v3),
         jnp.broadcast_to(scale, (1, 128)), jnp.zeros((1, 128), F32)], axis=0)

    def t_copy(k, src):
        return remote(tiles.at[src], tiles.at[src], t_ssem.at[k], t_rsem.at[k], (e, lax.rem(s + k, SHARDS)))

    loop(1, SHARDS, lambda k: t_copy(k, s).start())
    loop(1, CHIPS, lambda k: av_copy(k, chip(k)).start())
    pending["av"] = lambda: loop(1, CHIPS, lambda k: av_copy(k, chip(k)).wait_send())
    pending["av in"] = lambda: loop(1, CHIPS, lambda k: av_in(k, from_chip(k)).wait_recv())
    pending["t"] = lambda: loop(1, SHARDS, lambda k: t_copy(k, s).wait_send())
    loop(1, SHARDS, lambda k: t_copy(k, lax.rem(s + SHARDS - k, SHARDS)).wait_recv())

    every = tiles[...]
    scales = every[:, 6:7, :]
    top = jnp.max(scales, axis=0, keepdims=True)
    ratio = jnp.broadcast_to(scales / top, every.shape)
    which = lax.broadcasted_iota(jnp.int32, every.shape, 1)
    power = ratio
    weight = jnp.where(which == 0, power, 0.0)
    for k in range(1, 6):
        power = power * ratio
        weight = jnp.where(which == k, power, weight)
    moments = jnp.sum(jnp.sum(every * weight, axis=0), axis=1, keepdims=True)
    m = [None] + [moments[k:k + 1] for k in range(6)]
    top = top[0, :, 0:1]
    coef = step_scalars(m, EPS / top, EPS / top / top)
    rel = scale / top
    coef = [coef[0], coef[1] * rel, coef[2] * rel * rel]
    total = coef[0] * r0 + coef[1] * v1 + coef[2] * v2
    mine[...] = (FACTOR / top * total).astype(BF16)

    own_copy = pltpu.make_async_copy(mine, sg.at[p, c], own_sem)
    own_copy.start()

    def s_copy(k):
        return remote(mine, sg.at[p, c], s_ssem.at[k], s_rsem.at[k], (e, 2 * chip(k) + c))

    def s_in(k, q):
        return remote(mine, sg.at[q, c], s_ssem.at[k], s_rsem.at[k], (e, 2 * chip(k) + c))

    def sf_copy(k, q):
        return remote(sg.at[q, c], sg.at[q, c], sf_ssem.at[k], sf_rsem.at[k], sib)

    def sf_wait(k, q):
        remote(sg.at[q, 1 - c], sg.at[q, 1 - c], sf_ssem.at[k], sf_rsem.at[k], sib).wait_recv()

    own_share = remote(mine, sg.at[p, c], sf_ssem.at[0], sf_rsem.at[0], sib)
    own_share.start()
    loop(1, CHIPS, lambda k: s_copy(k).start())
    pending["s"] = lambda: loop(1, CHIPS, lambda k: s_copy(k).wait_send())
    pending["sf"] = lambda: (own_share.wait_send(), loop(1, CHIPS, lambda k: sf_copy(k, from_chip(k)).wait_send()))
    pending["own"] = own_copy.wait

    last = r0 - rel * (coef[0] * v1 + coef[1] * v2 + coef[2] * v3)

    def add_av(k, carry):
        q = from_chip(k)
        av_in(k, q).wait_recv()
        return carry + av[q].astype(F32)

    pending.pop("av in")
    whole = lax.fori_loop(1, CHIPS, add_av, stage[p, PACKED + 128:].astype(F32))
    fit[...] = (whole - last).astype(BF16)
    returns = []
    for at, d in enumerate(ORDER):
        if d:
            back_copy = remote(fit.at[pl.ds(at * CAP, CAP)], ret.at[pl.ds(d * CAP, CAP)], r_ssem.at[d], r_rsem.at[d], (back(d), s))
            back_copy.start()
            returns.append(back_copy)
        else:
            ret[0:CAP] = fit[at * CAP:(at + 1) * CAP]

    def share_step(k):
        q = from_chip(k)
        s_in(k, q).wait_recv()
        sf_copy(k, q).start()

    loop(1, CHIPS, share_step)

    for back_copy in returns:
        back_copy.wait()
    refit_ref[...] = lax.dot_general(combining, ret[...].astype(F32), (((0,), (0,)), ((), ())),
                                     precision=lax.Precision.HIGHEST, preferred_element_type=F32).astype(BF16)
    loop(0, CHIPS, lambda k: sf_wait(k, from_chip(k)))
    finish()


PIECES = 4


def apply_kernel(sg_hbm, ht_hbm, refit_hbm, down_hbm, kept_hbm, refit_ref, new_hbm, sg, ht, down, kept, new, sem, out_sem):
    wide = DW // PIECES
    chips = CHIPS // PIECES

    def cols(i):
        return pl.ds(i * wide, wide)

    small = [pltpu.make_async_copy(a, b, sem.at[i]) for i, (a, b) in enumerate([(ht_hbm, ht), (kept_hbm, kept), (refit_hbm, refit_ref)])]
    parts = []
    for i in range(PIECES):
        parts.append((
            pltpu.make_async_copy(sg_hbm.at[pl.ds(i * chips, chips)], sg.at[pl.ds(i * chips, chips)], sem.at[3 + 2 * i]),
            pltpu.make_async_copy(down_hbm.at[0, :, cols(i)], down.at[:, cols(i)], sem.at[4 + 2 * i])))
    for copy in small[:2] + [copy for part in parts for copy in part] + small[2:]:
        copy.start()
    small[0].wait()
    small[1].wait()
    h = ht[...]
    row = lax.broadcasted_iota(jnp.int32, (2, 128), 0)
    keeps = [dot(kept[0].astype(F32), (row == f).astype(F32), 0, 0) for f in range(2)]
    writes = []
    for i in range(PIECES):
        for copy in parts[i]:
            copy.wait()
        for n in range(2 * chips):
            j = 2 * chips * i + n
            at = slice(j * 128, (j + 1) * 128)
            w = dot(h, sg[j // 2, j % 2]) + down[:, at].astype(F32)
            new[:128, at] = (w[:128] * keeps[0][j:j + 1]).astype(BF16)
            new[128:, at] = (w[128:] * keeps[1][j:j + 1]).astype(BF16)
        write = pltpu.make_async_copy(new.at[:, cols(i)], new_hbm.at[0, :, cols(i)], out_sem.at[i])
        write.start()
        writes.append(write)
    for copy in writes + small[2:]:
        copy.wait()


def body(tokens, routes, router_logits, gate_weight, up_weight, down_weight, kept_blocks):
    rows, model = tokens.shape
    width = model * 2 // (3 * CHIPS)
    direct = model // 3
    own = gate_weight.shape[2]
    dma = pltpu.SemaphoreType.DMA
    vmem = pl.BlockSpec(memory_space=pltpu.VMEM)
    hbm = pl.BlockSpec(memory_space=pltpu.HBM)
    gathered, turned, refit = pl.pallas_call(
        kernel,
        out_shape=(jax.ShapeDtypeStruct((CHIPS, 2, 128, 128), BF16), jax.ShapeDtypeStruct((own, ROWS), BF16),
                   jax.ShapeDtypeStruct((rows, DW // SHARDS), BF16)),
        in_specs=[hbm] * 7,
        out_specs=(hbm, vmem, vmem),
        scratch_shapes=[
            pltpu.VMEM((rows, width), BF16),
            pltpu.VMEM((rows, direct), BF16),
            pltpu.VMEM((2, rows), jnp.int32),
            pltpu.VMEM((2, rows), F32),
            pltpu.VMEM(kept_blocks.shape, jnp.int32),
            pltpu.VMEM((model, own), BF16),
            pltpu.VMEM((model, own), BF16),
            pltpu.VMEM((own, DW), BF16),
            pltpu.VMEM((ROWS, width), BF16),
            pltpu.VMEM((ROWS, direct), BF16),
            pltpu.VMEM((CHIPS, 2, ROWS // 2, width), BF16),
            pltpu.VMEM((2, ROWS // 2, direct), BF16),
            pltpu.VMEM((ROWS, own), F32),
            pltpu.VMEM((ROWS, own), F32),
            pltpu.VMEM((ROWS, own), BF16),
            pltpu.VMEM((ROWS, own), BF16),
            pltpu.VMEM((CHIPS, own, 128), BF16),
            pltpu.VMEM((2, SHARDS, 128), F32),
            pltpu.VMEM((2, SHARDS, 128), F32),
            pltpu.VMEM((4, PACKED, 128), F32),
            pltpu.VMEM((CHIPS, PACKED + 256, 128), BF16),
            pltpu.VMEM((CHIPS, PACKED + 128, 128), BF16),
            pltpu.VMEM((CHIPS, 128, 128), BF16),
            pltpu.VMEM((SHARDS, 8, 128), F32),
            pltpu.VMEM((ROWS, 128), BF16),
            pltpu.VMEM((ROWS, 128), BF16),
            pltpu.VMEM((ROWS, 128), BF16),
            dma((8,)),
            dma((4,)), dma((4,)),
            dma((4,)), dma((4,)),
            dma((4,)), dma((4,)),
            dma((CHIPS,)), dma((CHIPS,)),
            dma((CHIPS,)), dma((CHIPS,)),
            dma((CHIPS,)), dma((CHIPS,)),
            dma((2,)), dma((2,)),
            dma((CHIPS,)), dma((CHIPS,)),
            dma((CHIPS,)), dma((CHIPS,)),
            dma((SHARDS,)), dma((SHARDS,)),
            dma((CHIPS,)), dma((CHIPS,)),
            dma((CHIPS,)), dma((CHIPS,)),
            dma((GROUPS,)), dma((GROUPS,)),
            dma,
        ],
        compiler_params=pltpu.CompilerParams(collective_id=0, has_side_effects=True, vmem_limit_bytes=60 << 20),
        name="refit",
    )(tokens, routes.T, router_logits.T, gate_weight, up_weight, down_weight, kept_blocks)
    return pl.pallas_call(
        apply_kernel,
        out_shape=(jax.ShapeDtypeStruct(refit.shape, BF16), jax.ShapeDtypeStruct(down_weight.shape, BF16)),
        in_specs=[hbm] * 5,
        out_specs=(vmem, hbm),
        scratch_shapes=[
            pltpu.VMEM(gathered.shape, BF16),
            pltpu.VMEM(turned.shape, BF16),
            pltpu.VMEM((own, DW), BF16),
            pltpu.VMEM(kept_blocks.shape, jnp.int32),
            pltpu.VMEM((own, DW), BF16),
            dma((3 + 2 * PIECES,)),
            dma((PIECES,)),
        ],
        compiler_params=pltpu.CompilerParams(vmem_limit_bytes=60 << 20),
        name="apply",
    )(gathered, turned, refit, down_weight, kept_blocks)


def solution(mesh):
    in_specs = (
        P("expert", None),
        P("expert", None),
        P("expert", None),
        P("expert", None, "shard"),
        P("expert", None, "shard"),
        P("expert", "shard", None),
        P("expert", "shard", None),
    )
    out_specs = (P("expert", "shard"), P("expert", "shard", None))
    return jax.shard_map(body, mesh=mesh, in_specs=in_specs, out_specs=out_specs, check_vma=False)
```

```python
import functools

import jax
import jax.numpy as jnp
from jax import lax
from jax.experimental import pallas as pl
from jax.experimental.pallas import tpu as pltpu
from jax.sharding import PartitionSpec as P

FF = 8192
DW = 4096
EPS = 1e-6
FACTOR = FF ** -0.5
CAP = 16
GROUPS = 8
CHIPS = 16
SHARDS = 32
ROWS = GROUPS * CAP
PACKED = 96
HALF = (PACKED + 128) // 2
TINY = 1e-30
MESH = pl.DeviceIdType.MESH
F32 = jnp.float32
BF16 = jnp.bfloat16

ORDER = (1, 3, 5, 7, 0, 2, 4, 6)


def dot(a, b, ca=1, cb=0):
    return lax.dot_general(a, b, (((ca,), (cb,)), ((), ())), preferred_element_type=F32)


def slot_rows(routes, plane):
    rel = [lax.rem(routes[k:k + 1] - plane + GROUPS, GROUPS) for k in range(2)]
    tok = rel[0].shape[1]
    experts = lax.broadcasted_iota(jnp.int32, (GROUPS, tok), 0)
    onehot = [(r == experts).astype(F32) for r in rel]
    earlier = lax.broadcasted_iota(jnp.int32, (tok, tok), 0) < lax.broadcasted_iota(jnp.int32, (tok, tok), 1)
    before = dot((onehot[0] + onehot[1]).astype(BF16), earlier.astype(BF16))
    slots = [jnp.sum(before * o, axis=0, keepdims=True) for o in onehot]
    rows = lax.broadcasted_iota(jnp.int32, (ROWS, tok), 0).astype(F32)
    return [(r * CAP).astype(F32) + s == rows for r, s in zip(rel, slots)]


def packed(m):
    return jnp.concatenate([m[:64], jnp.concatenate([m[64:96, 64:], m[96:, 64:]], axis=1)], axis=0)


def unpacked(m):
    corner = jnp.concatenate([m[64:, :64], m[64:, 64:]], axis=0)
    return jnp.concatenate([m[:64], jnp.concatenate([jnp.transpose(m[:64])[64:], corner], axis=1)], axis=0)


def step_scalars(m, eps1, eps2):
    def form(p, shift):
        total = None
        size = None
        for i, a in enumerate(p):
            for j, b in enumerate(p):
                term = a * b * m[i + j + shift]
                total = term if total is None else total + term
                size = jnp.abs(term) if size is None else size + jnp.abs(term)
        return jnp.maximum(total, 0.0), size

    one = jnp.ones_like(m[1])
    r, s = [one], [one]
    gnorm, _ = form(r, 1)
    out = None
    for it in range(3):
        image, size = form(s, 2)
        image = jnp.maximum(image, 1e-6 * size)
        step = gnorm / (image + eps2)
        term = [step * a for a in s]
        out = term if out is None else [a + b for a, b in zip(out + [0.0] * (len(term) - len(out)), term)]
        if it < 2:
            r = [a - b for a, b in zip(r + [0.0], [0.0] + term)]
            fresh, _ = form(r, 1)
            beta = fresh / (gnorm + eps1)
            s = [a + b for a, b in zip(r, [beta * c for c in s] + [0.0])]
            gnorm = fresh
    return out


def kernel(tok_hbm, routes_hbm, logits_hbm, gate_hbm, up_hbm, down_hbm, kept_hbm,
           sg, ht, refit_ref,
           tok, tokd, routes, logits, kept, gate, up, down, outgoing, outd, xg, xd, acc_g, acc_u, hown, hsib, vsib, kb, ksib, gram,
           stage, one, relay, two, av, tiles, mine, fit, ret,
           load_sem, z_ssem, z_rsem, d_ssem, d_rsem, df_ssem, df_rsem, ag_ssem, ag_rsem, fw_ssem, fw_rsem, v_ssem, v_rsem, k_sem, h_sem,
           one_ssem, one_rsem, two_ssem, two_rsem, av_ssem, av_rsem, t_ssem, t_rsem, s_ssem, s_rsem, sf_ssem, sf_rsem, r_ssem, r_rsem, own_sem):
    e = lax.axis_index("expert")
    s = lax.axis_index("shard")
    p = s // 2
    c = lax.rem(s, 2)
    sib = (e, 2 * p + 1 - c)
    width = tok.shape[1]
    direct = tokd.shape[1]
    planar = CHIPS * width

    def offset(k):
        j = lax.rem(7 * k, CHIPS)
        return j // 4, lax.rem(j, 4)

    def chip(k):
        dy, dx = offset(k)
        return 4 * lax.rem(p // 4 + dy, 4) + lax.rem(lax.rem(p, 4) + dx, 4)

    def from_chip(k):
        dy, dx = offset(k)
        return 4 * lax.rem(p // 4 + 4 - dy, 4) + lax.rem(lax.rem(p, 4) + 4 - dx, 4)

    def plane(d):
        return lax.rem(e + d, GROUPS)

    def back(d):
        return lax.rem(e + GROUPS - d, GROUPS)

    def remote(src, dst, ssem, rsem, device):
        return pltpu.make_async_remote_copy(src_ref=src, dst_ref=dst, send_sem=ssem, recv_sem=rsem,
                                            device_id=device, device_id_type=MESH)

    def loop(lo, hi, f):
        lax.fori_loop(lo, hi, lambda k, _: (f(k), 0)[1], 0)

    pending = {}

    def finish():
        for name in list(pending):
            pending.pop(name)()

    barrier = pltpu.get_barrier_semaphore()
    loop(1, GROUPS, lambda d: pl.semaphore_signal(barrier, inc=1, device_id=(plane(d), s), device_id_type=MESH))
    loop(1, SHARDS, lambda k: pl.semaphore_signal(barrier, inc=1, device_id=(e, lax.rem(s + k, SHARDS)), device_id_type=MESH))

    loads = [
        pltpu.make_async_copy(tok_hbm.at[:, pl.ds(pl.multiple_of(p * width, 128), width)], tok, load_sem.at[0]),
        pltpu.make_async_copy(routes_hbm, routes, load_sem.at[1]),
        pltpu.make_async_copy(logits_hbm, logits, load_sem.at[2]),
        pltpu.make_async_copy(kept_hbm, kept, load_sem.at[3]),
        pltpu.make_async_copy(gate_hbm.at[0], gate, load_sem.at[4]),
        pltpu.make_async_copy(up_hbm.at[0], up, load_sem.at[5]),
        pltpu.make_async_copy(down_hbm.at[0], down, load_sem.at[6]),
        pltpu.make_async_copy(tok_hbm.at[:, pl.ds(planar, direct)], tokd, load_sem.at[7]),
    ]
    for load in [loads[0], loads[7]] + loads[1:7]:
        load.start()

    for load in loads[:4]:
        load.wait()
    match = slot_rows(routes[...], e)
    placing = (match[0] | match[1]).astype(BF16)
    outgoing[...] = dot(placing, tok[...]).astype(BF16)
    loads[7].wait()
    outd[...] = dot(placing, tokd[...]).astype(BF16)
    logit = logits[0:1] - logits[1:2]
    share = 1.0 / (1.0 + jnp.exp(-logit))
    combining = jnp.where(match[0], share, 0.0) + jnp.where(match[1], 1.0 - share, 0.0)
    row = lax.broadcasted_iota(jnp.int32, (2, 128), 0)
    for f in range(2):
        kb[f] = dot(kept[0].astype(F32), (row == f).astype(F32), 0, 0)

    pending["loads"] = lambda: [load.wait() for load in loads[4:7]]
    pl.semaphore_wait(barrier, GROUPS - 1 + SHARDS - 1)

    def slots(i):
        return pl.ds(pl.multiple_of(i * CAP, CAP), CAP)

    def z_copy(i):
        d = 2 * i + 1 - c
        return remote(outgoing.at[slots(d)], xg.at[p, c, slots(i)], z_ssem.at[i], z_rsem.at[i], (plane(d), s))

    def d_copy(i):
        d = 2 * i + 1 - c
        return remote(outd.at[slots(d)], xd.at[c, slots(i)], d_ssem.at[i], d_rsem.at[i], (plane(d), s))

    @pl.when(c == 0)
    def _():
        z_copy(0).start()

    loop(1, 4, lambda i: z_copy(i).start())

    @pl.when(c == 0)
    def _():
        d_copy(0).start()

    loop(1, 4, lambda i: d_copy(i).start())

    @pl.when(c == 1)
    def _():
        xg[p, 1, 0:CAP] = outgoing[0:CAP]
        xd[1, 0:CAP] = outd[0:CAP]

    def z_sent():
        @pl.when(c == 0)
        def _():
            z_copy(0).wait_send()
            d_copy(0).wait_send()

        loop(1, 4, lambda i: z_copy(i).wait_send())
        loop(1, 4, lambda i: d_copy(i).wait_send())

    def z_arrived():
        @pl.when(c == 0)
        def _():
            z_copy(0).wait_recv()

        loop(1, 4, lambda i: z_copy(i).wait_recv())

    pending["z"] = z_sent

    def v_copy(q):
        return remote(down_hbm.at[0, :, pl.ds(pl.multiple_of((2 * q + 1 - c) * 128, 128), 128)], vsib.at[q],
                      v_ssem.at[q], v_rsem.at[q], sib)

    loop(0, CHIPS, lambda q: v_copy(q).start())
    k_copy = remote(kb, ksib, k_sem.at[0], k_sem.at[1], sib)
    k_copy.start()
    pending["v"] = lambda: loop(0, CHIPS, lambda q: v_copy(q).wait())
    pending["k"] = k_copy.wait
    z_arrived()

    def ag_copy(k, q):
        return remote(xg.at[q, c], xg.at[q, c], ag_ssem.at[k], ag_rsem.at[k], (e, 2 * chip(k) + c))

    def fw_copy(k, q):
        return remote(xg.at[q, c], xg.at[q, c], fw_ssem.at[k], fw_rsem.at[k], sib)

    def fw_wait(k, q):
        remote(xg.at[q, 1 - c], xg.at[q, 1 - c], fw_ssem.at[k], fw_rsem.at[k], sib).wait_recv()

    loop(1, CHIPS, lambda k: ag_copy(k, p).start())
    fw_copy(0, p).start()
    pending["ag"] = lambda: loop(1, CHIPS, lambda k: ag_copy(k, p).wait_send())

    def df_copy(i):
        return remote(xd.at[c, slots(i)], xd.at[c, slots(i)], df_ssem.at[i], df_rsem.at[i], sib)

    def df_wait(i):
        remote(xd.at[1 - c, slots(i)], xd.at[1 - c, slots(i)], df_ssem.at[i], df_rsem.at[i], sib).wait_recv()

    @pl.when(c == 0)
    def _():
        d_copy(0).wait_recv()

    df_copy(0).start()

    def direct_step(i):
        d_copy(i).wait_recv()
        df_copy(i).start()

    loop(1, 4, direct_step)
    pending["df"] = lambda: loop(0, 4, lambda i: df_copy(i).wait_send())
    pending["fw"] = lambda: loop(0, CHIPS, lambda k: fw_copy(k, from_chip(k)).wait_send())
    pending.pop("loads")()
    acc_g[...] = jnp.zeros_like(acc_g)
    acc_u[...] = jnp.zeros_like(acc_u)

    def expand(k):
        q = from_chip(k)
        fw_wait(k, q)
        x = xg[q].reshape(ROWS, width)
        rows = pl.ds(pl.multiple_of(q * width, 128), width)
        acc_g[...] += dot(x, gate[rows, :])
        acc_u[...] += dot(x, up[rows, :])

    def expand_direct(n):
        x = xd[:, :, pl.ds(pl.multiple_of(n * width, 128), width)].reshape(ROWS, width)
        rows = pl.ds(pl.multiple_of(planar + n * width, 128), width)
        acc_g[...] += dot(x, gate[rows, :])
        acc_u[...] += dot(x, up[rows, :])

    def gather_step(k):
        q = from_chip(k)
        ag_copy(k, q).wait_recv()
        fw_copy(k, q).start()

    half = direct // width
    gather_step(1)
    loop(0, 4, df_wait)
    expand_direct(0)

    def early(k):
        gather_step(k)
        expand_direct(k - 1)

    def late(k):
        gather_step(k)
        expand(2 * (k - half - 1))
        expand(2 * (k - half - 1) + 1)

    loop(2, half + 1, early)
    loop(half + 1, CHIPS, late)
    loop(2 * (CHIPS - half - 1), CHIPS, expand)
    g = acc_g[...]
    h32 = g / (1.0 + jnp.exp(-g)) * acc_u[...]
    hown[...] = h32.astype(BF16)
    h_copy = remote(hown, hsib, h_sem.at[0], h_sem.at[1], sib)
    h_copy.start()
    ht[...] = jnp.transpose(hown[...].astype(F32)).astype(BF16)

    def grams(h, base):
        for f in range(2):
            hf = h[:, f * 128:(f + 1) * 128]
            gram[base + f] = packed(FACTOR * FACTOR * dot(hf, hf, 1, 1))

    grams(hown[...], 0)
    pending.pop("v")()
    pending.pop("k")()
    h_copy.wait()
    grams(hsib[...], 2)

    def masked(v, k0, k1):
        return jnp.concatenate([v[:128] * (1.0 - k0).astype(BF16), v[128:] * (1.0 - k1).astype(BF16)], axis=0)

    def av_copy(k, q):
        return remote(stage.at[q, pl.ds(PACKED + 128, 128)], av.at[p], av_ssem.at[k], av_rsem.at[k], (e, 2 * q + c))

    def partial(q):
        j = 2 * q + c
        ko = [kb[f, pl.ds(j, 1), :] for f in range(2)]
        ks = [ksib[f, pl.ds(j, 1), :] for f in range(2)]
        stage[q, 0:PACKED] = (ko[0] * gram[0] + ko[1] * gram[1] + ks[0] * gram[2] + ks[1] * gram[3]).astype(BF16)
        vo = down[:, pl.ds(pl.multiple_of(j * 128, 128), 128)]
        vs = vsib[q]
        both = dot(hown[...], jnp.concatenate([masked(vo, *ko), vo], axis=1))
        both += dot(hsib[...], jnp.concatenate([masked(vs, *ks), vs], axis=1))
        both = (FACTOR * both).astype(BF16)
        stage[q, PACKED:PACKED + 128] = both[:, :128]
        stage[q, PACKED + 128:] = both[:, 128:]

    def across(dy, dx):
        return 4 * lax.rem(p // 4 + dy, 4) + lax.rem(lax.rem(p, 4) + dx, 4)

    def first(way, far, step):
        q = across(far, step) if way == 0 else across(step, far)
        to = across(0, step) if way == 0 else across(step, 0)
        i = 4 * (step - 1) + far
        return remote(stage.at[q, pl.ds(way * HALF, HALF)], one.at[way, i], one_ssem.at[way, i], one_rsem.at[way, i], (e, 2 * to + c))

    def second(way, far):
        to = across(far, 0) if way == 0 else across(0, far)
        return remote(relay.at[way, far - 1], two.at[way, far - 1], two_ssem.at[way, far - 1], two_rsem.at[way, far - 1], (e, 2 * to + c))

    def send_far(n):
        dy, dx = n // 3 + 1, lax.rem(n, 3) + 1
        partial(across(dy, dx))
        first(0, dy, dx).start()
        first(1, dx, dy).start()

    def send_near(d):
        partial(across(0, d))
        first(0, 0, d).start()
        partial(across(d, 0))
        first(1, 0, d).start()

    loop(0, 9, send_far)
    loop(1, 4, send_near)
    partial(p)

    def firsts_sent(n):
        far, step = lax.rem(n, 4), n // 4 + 1
        first(0, far, step).wait_send()
        first(1, far, step).wait_send()

    pending["one"] = lambda: loop(0, 12, firsts_sent)

    def gathered(way, far):
        q = across(far, 0) if way == 0 else across(0, far)
        total = stage[q, way * HALF:(way + 1) * HALF].astype(F32)
        for step in range(1, 4):
            first(way, far, step).wait_recv()
            total += one[way, 4 * (step - 1) + far].astype(F32)
        return total

    for far in range(1, 4):
        for way in range(2):
            relay[way, far - 1] = gathered(way, far).astype(BF16)
            second(way, far).start()

    pending["two"] = lambda: [second(way, far).wait_send() for way in range(2) for far in range(1, 4)]
    halves = [gathered(way, 0) for way in range(2)]
    for far in range(1, 4):
        for way in range(2):
            second(way, far).wait_recv()
            halves[way] += two[way, far - 1].astype(F32)

    summed = jnp.concatenate(halves, axis=0)
    big, r0 = unpacked(summed[:PACKED]), summed[PACKED:]

    def av_in(k, q):
        return remote(stage.at[p, pl.ds(PACKED + 128, 128)], av.at[q], av_ssem.at[k], av_rsem.at[k], (e, 2 * q + c))


    eye = lax.broadcasted_iota(jnp.int32, (128, 128), 0) == lax.broadcasted_iota(jnp.int32, (128, 128), 1)
    scale = jnp.sum(jnp.sum(jnp.where(eye, big, 0.0), axis=0, keepdims=True), axis=1, keepdims=True)
    scale = jnp.maximum(scale, TINY)
    mb = (big / scale).astype(BF16)

    def apply(v):
        hi = v.astype(BF16)
        lo = (v - hi.astype(F32)).astype(BF16)
        w = dot(mb, jnp.concatenate([hi, lo], axis=1))
        return w[:, :128] + w[:, 128:]

    v1 = apply(r0)
    v2 = apply(v1)
    v3 = apply(v2)

    def inner(a, b):
        return jnp.sum(a * b, axis=0, keepdims=True)

    tiles[s] = jnp.concatenate(
        [inner(r0, v1), inner(v1, v1), inner(v1, v2), inner(v2, v2), inner(v2, v3), inner(v3, v3),
         jnp.broadcast_to(scale, (1, 128)), jnp.zeros((1, 128), F32)], axis=0)

    def t_copy(k, src):
        return remote(tiles.at[src], tiles.at[src], t_ssem.at[k], t_rsem.at[k], (e, lax.rem(s + k, SHARDS)))

    loop(1, SHARDS, lambda k: t_copy(k, s).start())
    loop(1, CHIPS, lambda k: av_copy(k, chip(k)).start())
    pending["av"] = lambda: loop(1, CHIPS, lambda k: av_copy(k, chip(k)).wait_send())
    pending["av in"] = lambda: loop(1, CHIPS, lambda k: av_in(k, from_chip(k)).wait_recv())
    pending["t"] = lambda: loop(1, SHARDS, lambda k: t_copy(k, s).wait_send())
    loop(1, SHARDS, lambda k: t_copy(k, lax.rem(s + SHARDS - k, SHARDS)).wait_recv())

    every = tiles[...]
    scales = every[:, 6:7, :]
    top = jnp.max(scales, axis=0, keepdims=True)
    ratio = jnp.broadcast_to(scales / top, every.shape)
    which = lax.broadcasted_iota(jnp.int32, every.shape, 1)
    power = ratio
    weight = jnp.where(which == 0, power, 0.0)
    for k in range(1, 6):
        power = power * ratio
        weight = jnp.where(which == k, power, weight)
    moments = jnp.sum(jnp.sum(every * weight, axis=0), axis=1, keepdims=True)
    m = [None] + [moments[k:k + 1] for k in range(6)]
    top = top[0, :, 0:1]
    coef = step_scalars(m, EPS / top, EPS / top / top)
    rel = scale / top
    coef = [coef[0], coef[1] * rel, coef[2] * rel * rel]
    total = coef[0] * r0 + coef[1] * v1 + coef[2] * v2
    mine[...] = (FACTOR / top * total).astype(BF16)

    own_copy = pltpu.make_async_copy(mine, sg.at[p, c], own_sem)
    own_copy.start()

    def s_copy(k):
        return remote(mine, sg.at[p, c], s_ssem.at[k], s_rsem.at[k], (e, 2 * chip(k) + c))

    def s_in(k, q):
        return remote(mine, sg.at[q, c], s_ssem.at[k], s_rsem.at[k], (e, 2 * chip(k) + c))

    def sf_copy(k, q):
        return remote(sg.at[q, c], sg.at[q, c], sf_ssem.at[k], sf_rsem.at[k], sib)

    def sf_wait(k, q):
        remote(sg.at[q, 1 - c], sg.at[q, 1 - c], sf_ssem.at[k], sf_rsem.at[k], sib).wait_recv()

    own_share = remote(mine, sg.at[p, c], sf_ssem.at[0], sf_rsem.at[0], sib)
    own_share.start()
    loop(1, CHIPS, lambda k: s_copy(k).start())
    pending["s"] = lambda: loop(1, CHIPS, lambda k: s_copy(k).wait_send())
    pending["sf"] = lambda: (own_share.wait_send(), loop(1, CHIPS, lambda k: sf_copy(k, from_chip(k)).wait_send()))
    pending["own"] = own_copy.wait

    last = r0 - rel * (coef[0] * v1 + coef[1] * v2 + coef[2] * v3)

    def add_av(k, carry):
        q = from_chip(k)
        av_in(k, q).wait_recv()
        return carry + av[q].astype(F32)

    pending.pop("av in")
    whole = lax.fori_loop(1, CHIPS, add_av, stage[p, PACKED + 128:].astype(F32))
    fit[...] = (whole - last).astype(BF16)
    returns = []
    for at, d in enumerate(ORDER):
        if d:
            back_copy = remote(fit.at[pl.ds(at * CAP, CAP)], ret.at[pl.ds(d * CAP, CAP)], r_ssem.at[d], r_rsem.at[d], (back(d), s))
            back_copy.start()
            returns.append(back_copy)
        else:
            ret[0:CAP] = fit[at * CAP:(at + 1) * CAP]

    def share_step(k):
        q = from_chip(k)
        s_in(k, q).wait_recv()
        sf_copy(k, q).start()

    loop(1, CHIPS, share_step)

    for back_copy in returns:
        back_copy.wait()
    refit_ref[...] = lax.dot_general(combining, ret[...].astype(F32), (((0,), (0,)), ((), ())),
                                     precision=lax.Precision.HIGHEST, preferred_element_type=F32).astype(BF16)
    loop(0, CHIPS, lambda k: sf_wait(k, from_chip(k)))
    finish()


PIECES = 4


def apply_kernel(sg_hbm, ht_hbm, refit_hbm, down_hbm, kept_hbm, refit_ref, new_hbm, sg, ht, down, kept, new, sem, out_sem):
    wide = DW // PIECES
    chips = CHIPS // PIECES

    def cols(i):
        return pl.ds(i * wide, wide)

    small = [pltpu.make_async_copy(a, b, sem.at[i]) for i, (a, b) in enumerate([(ht_hbm, ht), (kept_hbm, kept), (refit_hbm, refit_ref)])]
    parts = []
    for i in range(PIECES):
        parts.append((
            pltpu.make_async_copy(sg_hbm.at[pl.ds(i * chips, chips)], sg.at[pl.ds(i * chips, chips)], sem.at[3 + 2 * i]),
            pltpu.make_async_copy(down_hbm.at[0, :, cols(i)], down.at[:, cols(i)], sem.at[4 + 2 * i])))
    for copy in small[:2] + [copy for part in parts for copy in part] + small[2:]:
        copy.start()
    small[0].wait()
    small[1].wait()
    h = ht[...]
    row = lax.broadcasted_iota(jnp.int32, (2, 128), 0)
    keeps = [dot(kept[0].astype(F32), (row == f).astype(F32), 0, 0) for f in range(2)]
    writes = []
    for i in range(PIECES):
        for copy in parts[i]:
            copy.wait()
        for n in range(2 * chips):
            j = 2 * chips * i + n
            at = slice(j * 128, (j + 1) * 128)
            w = dot(h, sg[j // 2, j % 2]) + down[:, at].astype(F32)
            new[:128, at] = (w[:128] * keeps[0][j:j + 1]).astype(BF16)
            new[128:, at] = (w[128:] * keeps[1][j:j + 1]).astype(BF16)
        write = pltpu.make_async_copy(new.at[:, cols(i)], new_hbm.at[0, :, cols(i)], out_sem.at[i])
        write.start()
        writes.append(write)
    for copy in writes + small[2:]:
        copy.wait()


def body(tokens, routes, router_logits, gate_weight, up_weight, down_weight, kept_blocks):
    rows, model = tokens.shape
    width = model * 2 // (3 * CHIPS)
    direct = model // 3
    own = gate_weight.shape[2]
    dma = pltpu.SemaphoreType.DMA
    vmem = pl.BlockSpec(memory_space=pltpu.VMEM)
    hbm = pl.BlockSpec(memory_space=pltpu.HBM)
    gathered, turned, refit = pl.pallas_call(
        kernel,
        out_shape=(jax.ShapeDtypeStruct((CHIPS, 2, 128, 128), BF16), jax.ShapeDtypeStruct((own, ROWS), BF16),
                   jax.ShapeDtypeStruct((rows, DW // SHARDS), BF16)),
        in_specs=[hbm] * 7,
        out_specs=(hbm, vmem, vmem),
        scratch_shapes=[
            pltpu.VMEM((rows, width), BF16),
            pltpu.VMEM((rows, direct), BF16),
            pltpu.VMEM((2, rows), jnp.int32),
            pltpu.VMEM((2, rows), F32),
            pltpu.VMEM(kept_blocks.shape, jnp.int32),
            pltpu.VMEM((model, own), BF16),
            pltpu.VMEM((model, own), BF16),
            pltpu.VMEM((own, DW), BF16),
            pltpu.VMEM((ROWS, width), BF16),
            pltpu.VMEM((ROWS, direct), BF16),
            pltpu.VMEM((CHIPS, 2, ROWS // 2, width), BF16),
            pltpu.VMEM((2, ROWS // 2, direct), BF16),
            pltpu.VMEM((ROWS, own), F32),
            pltpu.VMEM((ROWS, own), F32),
            pltpu.VMEM((ROWS, own), BF16),
            pltpu.VMEM((ROWS, own), BF16),
            pltpu.VMEM((CHIPS, own, 128), BF16),
            pltpu.VMEM((2, SHARDS, 128), F32),
            pltpu.VMEM((2, SHARDS, 128), F32),
            pltpu.VMEM((4, PACKED, 128), F32),
            pltpu.VMEM((CHIPS, PACKED + 256, 128), BF16),
            pltpu.VMEM((2, 12, HALF, 128), BF16),
            pltpu.VMEM((2, 3, HALF, 128), BF16),
            pltpu.VMEM((2, 3, HALF, 128), BF16),
            pltpu.VMEM((CHIPS, 128, 128), BF16),
            pltpu.VMEM((SHARDS, 8, 128), F32),
            pltpu.VMEM((ROWS, 128), BF16),
            pltpu.VMEM((ROWS, 128), BF16),
            pltpu.VMEM((ROWS, 128), BF16),
            dma((8,)),
            dma((4,)), dma((4,)),
            dma((4,)), dma((4,)),
            dma((4,)), dma((4,)),
            dma((CHIPS,)), dma((CHIPS,)),
            dma((CHIPS,)), dma((CHIPS,)),
            dma((CHIPS,)), dma((CHIPS,)),
            dma((2,)), dma((2,)),
            dma((2, 12)), dma((2, 12)),
            dma((2, 3)), dma((2, 3)),
            dma((CHIPS,)), dma((CHIPS,)),
            dma((SHARDS,)), dma((SHARDS,)),
            dma((CHIPS,)), dma((CHIPS,)),
            dma((CHIPS,)), dma((CHIPS,)),
            dma((GROUPS,)), dma((GROUPS,)),
            dma,
        ],
        compiler_params=pltpu.CompilerParams(collective_id=0, has_side_effects=True, vmem_limit_bytes=60 << 20),
        name="refit",
    )(tokens, routes.T, router_logits.T, gate_weight, up_weight, down_weight, kept_blocks)
    return pl.pallas_call(
        apply_kernel,
        out_shape=(jax.ShapeDtypeStruct(refit.shape, BF16), jax.ShapeDtypeStruct(down_weight.shape, BF16)),
        in_specs=[hbm] * 5,
        out_specs=(vmem, hbm),
        scratch_shapes=[
            pltpu.VMEM(gathered.shape, BF16),
            pltpu.VMEM(turned.shape, BF16),
            pltpu.VMEM((own, DW), BF16),
            pltpu.VMEM(kept_blocks.shape, jnp.int32),
            pltpu.VMEM((own, DW), BF16),
            dma((3 + 2 * PIECES,)),
            dma((PIECES,)),
        ],
        compiler_params=pltpu.CompilerParams(vmem_limit_bytes=60 << 20),
        name="apply",
    )(gathered, turned, refit, down_weight, kept_blocks)


def solution(mesh):
    in_specs = (
        P("expert", None),
        P("expert", None),
        P("expert", None),
        P("expert", None, "shard"),
        P("expert", None, "shard"),
        P("expert", "shard", None),
        P("expert", "shard", None),
    )
    out_specs = (P("expert", "shard"), P("expert", "shard", None))
    return jax.shard_map(body, mesh=mesh, in_specs=in_specs, out_specs=out_specs, check_vma=False)
```

```python
import functools

import jax
import jax.numpy as jnp
from jax import lax
from jax.experimental import pallas as pl
from jax.experimental.pallas import tpu as pltpu
from jax.sharding import PartitionSpec as P

FF = 8192
DW = 4096
EPS = 1e-6
FACTOR = FF ** -0.5
CAP = 16
GROUPS = 8
CHIPS = 16
SHARDS = 32
ROWS = GROUPS * CAP
PACKED = 96
HALF = (PACKED + 128) // 2
TINY = 1e-30
MESH = pl.DeviceIdType.MESH
F32 = jnp.float32
BF16 = jnp.bfloat16

ORDER = (1, 3, 5, 7, 0, 2, 4, 6)


def dot(a, b, ca=1, cb=0):
    return lax.dot_general(a, b, (((ca,), (cb,)), ((), ())), preferred_element_type=F32)


def slot_rows(routes, plane):
    rel = [lax.rem(routes[k:k + 1] - plane + GROUPS, GROUPS) for k in range(2)]
    tok = rel[0].shape[1]
    experts = lax.broadcasted_iota(jnp.int32, (GROUPS, tok), 0)
    onehot = [(r == experts).astype(F32) for r in rel]
    earlier = lax.broadcasted_iota(jnp.int32, (tok, tok), 0) < lax.broadcasted_iota(jnp.int32, (tok, tok), 1)
    before = dot((onehot[0] + onehot[1]).astype(BF16), earlier.astype(BF16))
    slots = [jnp.sum(before * o, axis=0, keepdims=True) for o in onehot]
    rows = lax.broadcasted_iota(jnp.int32, (ROWS, tok), 0).astype(F32)
    return [(r * CAP).astype(F32) + s == rows for r, s in zip(rel, slots)]


def packed(m):
    return jnp.concatenate([m[:64], jnp.concatenate([m[64:96, 64:], m[96:, 64:]], axis=1)], axis=0)


def unpacked(m):
    corner = jnp.concatenate([m[64:, :64], m[64:, 64:]], axis=0)
    return jnp.concatenate([m[:64], jnp.concatenate([jnp.transpose(m[:64])[64:], corner], axis=1)], axis=0)


def step_scalars(m, eps1, eps2):
    def form(p, shift):
        total = None
        size = None
        for i, a in enumerate(p):
            for j, b in enumerate(p):
                term = a * b * m[i + j + shift]
                total = term if total is None else total + term
                size = jnp.abs(term) if size is None else size + jnp.abs(term)
        return jnp.maximum(total, 0.0), size

    one = jnp.ones_like(m[1])
    r, s = [one], [one]
    gnorm, _ = form(r, 1)
    out = None
    for it in range(3):
        image, size = form(s, 2)
        image = jnp.maximum(image, 1e-6 * size)
        step = gnorm / (image + eps2)
        term = [step * a for a in s]
        out = term if out is None else [a + b for a, b in zip(out + [0.0] * (len(term) - len(out)), term)]
        if it < 2:
            r = [a - b for a, b in zip(r + [0.0], [0.0] + term)]
            fresh, _ = form(r, 1)
            beta = fresh / (gnorm + eps1)
            s = [a + b for a, b in zip(r, [beta * c for c in s] + [0.0])]
            gnorm = fresh
    return out


def kernel(tok_hbm, routes_hbm, logits_hbm, gate_hbm, up_hbm, down_hbm, kept_hbm,
           sg, ht_hbm, refit_hbm,
           tok, tokd, routes, logits, kept, gate, up, down, outgoing, outd, xg, xd, acc_g, acc_u, hown, hsib, ht, vsib, kb, ksib, gram,
           stage, one, relay, two, av, tiles, mine, fit, ret, refitted,
           load_sem, z_ssem, z_rsem, d_ssem, d_rsem, df_ssem, df_rsem, ag_ssem, ag_rsem, fw_ssem, fw_rsem, v_ssem, v_rsem, k_sem, h_sem,
           one_ssem, one_rsem, two_ssem, two_rsem, av_ssem, av_rsem, t_ssem, t_rsem, s_ssem, s_rsem, sf_ssem, sf_rsem, r_ssem, r_rsem, own_sem, ht_sem, refit_sem):
    e = lax.axis_index("expert")
    s = lax.axis_index("shard")
    p = s // 2
    c = lax.rem(s, 2)
    sib = (e, 2 * p + 1 - c)
    width = tok.shape[1]
    direct = tokd.shape[1]
    planar = CHIPS * width

    def offset(k):
        j = lax.rem(7 * k, CHIPS)
        return j // 4, lax.rem(j, 4)

    def chip(k):
        dy, dx = offset(k)
        return 4 * lax.rem(p // 4 + dy, 4) + lax.rem(lax.rem(p, 4) + dx, 4)

    def from_chip(k):
        dy, dx = offset(k)
        return 4 * lax.rem(p // 4 + 4 - dy, 4) + lax.rem(lax.rem(p, 4) + 4 - dx, 4)

    def plane(d):
        return lax.rem(e + d, GROUPS)

    def back(d):
        return lax.rem(e + GROUPS - d, GROUPS)

    def remote(src, dst, ssem, rsem, device):
        return pltpu.make_async_remote_copy(src_ref=src, dst_ref=dst, send_sem=ssem, recv_sem=rsem,
                                            device_id=device, device_id_type=MESH)

    def loop(lo, hi, f):
        lax.fori_loop(lo, hi, lambda k, _: (f(k), 0)[1], 0)

    pending = {}

    def finish():
        for name in list(pending):
            pending.pop(name)()

    barrier = pltpu.get_barrier_semaphore()
    loop(1, GROUPS, lambda d: pl.semaphore_signal(barrier, inc=1, device_id=(plane(d), s), device_id_type=MESH))
    loop(1, SHARDS, lambda k: pl.semaphore_signal(barrier, inc=1, device_id=(e, lax.rem(s + k, SHARDS)), device_id_type=MESH))

    loads = [
        pltpu.make_async_copy(tok_hbm.at[:, pl.ds(pl.multiple_of(p * width, 128), width)], tok, load_sem.at[0]),
        pltpu.make_async_copy(routes_hbm, routes, load_sem.at[1]),
        pltpu.make_async_copy(logits_hbm, logits, load_sem.at[2]),
        pltpu.make_async_copy(kept_hbm, kept, load_sem.at[3]),
        pltpu.make_async_copy(gate_hbm.at[0], gate, load_sem.at[4]),
        pltpu.make_async_copy(up_hbm.at[0], up, load_sem.at[5]),
        pltpu.make_async_copy(down_hbm.at[0], down, load_sem.at[6]),
        pltpu.make_async_copy(tok_hbm.at[:, pl.ds(planar, direct)], tokd, load_sem.at[7]),
    ]
    for load in [loads[0], loads[7]] + loads[1:7]:
        load.start()

    for load in loads[:4]:
        load.wait()
    match = slot_rows(routes[...], e)
    placing = (match[0] | match[1]).astype(BF16)
    outgoing[...] = dot(placing, tok[...]).astype(BF16)
    loads[7].wait()
    outd[...] = dot(placing, tokd[...]).astype(BF16)
    logit = logits[0:1] - logits[1:2]
    share = 1.0 / (1.0 + jnp.exp(-logit))
    combining = jnp.where(match[0], share, 0.0) + jnp.where(match[1], 1.0 - share, 0.0)
    row = lax.broadcasted_iota(jnp.int32, (2, 128), 0)
    for f in range(2):
        kb[f] = dot(kept[0].astype(F32), (row == f).astype(F32), 0, 0)

    pending["loads"] = lambda: [load.wait() for load in loads[4:7]]
    pl.semaphore_wait(barrier, GROUPS - 1 + SHARDS - 1)

    def slots(i):
        return pl.ds(pl.multiple_of(i * CAP, CAP), CAP)

    def z_copy(i):
        d = 2 * i + 1 - c
        return remote(outgoing.at[slots(d)], xg.at[p, c, slots(i)], z_ssem.at[i], z_rsem.at[i], (plane(d), s))

    def d_copy(i):
        d = 2 * i + 1 - c
        return remote(outd.at[slots(d)], xd.at[c, slots(i)], d_ssem.at[i], d_rsem.at[i], (plane(d), s))

    @pl.when(c == 0)
    def _():
        z_copy(0).start()

    loop(1, 4, lambda i: z_copy(i).start())

    @pl.when(c == 0)
    def _():
        d_copy(0).start()

    loop(1, 4, lambda i: d_copy(i).start())

    @pl.when(c == 1)
    def _():
        xg[p, 1, 0:CAP] = outgoing[0:CAP]
        xd[1, 0:CAP] = outd[0:CAP]

    def z_sent():
        @pl.when(c == 0)
        def _():
            z_copy(0).wait_send()
            d_copy(0).wait_send()

        loop(1, 4, lambda i: z_copy(i).wait_send())
        loop(1, 4, lambda i: d_copy(i).wait_send())

    def z_arrived():
        @pl.when(c == 0)
        def _():
            z_copy(0).wait_recv()

        loop(1, 4, lambda i: z_copy(i).wait_recv())

    pending["z"] = z_sent

    def v_copy(q):
        return remote(down_hbm.at[0, :, pl.ds(pl.multiple_of((2 * q + 1 - c) * 128, 128), 128)], vsib.at[q],
                      v_ssem.at[q], v_rsem.at[q], sib)

    loop(0, CHIPS, lambda q: v_copy(q).start())
    k_copy = remote(kb, ksib, k_sem.at[0], k_sem.at[1], sib)
    k_copy.start()
    pending["v"] = lambda: loop(0, CHIPS, lambda q: v_copy(q).wait())
    pending["k"] = k_copy.wait
    z_arrived()

    def ag_copy(k, q):
        return remote(xg.at[q, c], xg.at[q, c], ag_ssem.at[k], ag_rsem.at[k], (e, 2 * chip(k) + c))

    def fw_copy(k, q):
        return remote(xg.at[q, c], xg.at[q, c], fw_ssem.at[k], fw_rsem.at[k], sib)

    def fw_wait(k, q):
        remote(xg.at[q, 1 - c], xg.at[q, 1 - c], fw_ssem.at[k], fw_rsem.at[k], sib).wait_recv()

    loop(1, CHIPS, lambda k: ag_copy(k, p).start())
    fw_copy(0, p).start()
    pending["ag"] = lambda: loop(1, CHIPS, lambda k: ag_copy(k, p).wait_send())

    def df_copy(i):
        return remote(xd.at[c, slots(i)], xd.at[c, slots(i)], df_ssem.at[i], df_rsem.at[i], sib)

    def df_wait(i):
        remote(xd.at[1 - c, slots(i)], xd.at[1 - c, slots(i)], df_ssem.at[i], df_rsem.at[i], sib).wait_recv()

    @pl.when(c == 0)
    def _():
        d_copy(0).wait_recv()

    df_copy(0).start()

    def direct_step(i):
        d_copy(i).wait_recv()
        df_copy(i).start()

    loop(1, 4, direct_step)
    pending["df"] = lambda: loop(0, 4, lambda i: df_copy(i).wait_send())
    pending["fw"] = lambda: loop(0, CHIPS, lambda k: fw_copy(k, from_chip(k)).wait_send())
    pending.pop("loads")()
    acc_g[...] = jnp.zeros_like(acc_g)
    acc_u[...] = jnp.zeros_like(acc_u)

    def expand(k):
        q = from_chip(k)
        fw_wait(k, q)
        x = xg[q].reshape(ROWS, width)
        rows = pl.ds(pl.multiple_of(q * width, 128), width)
        acc_g[...] += dot(x, gate[rows, :])
        acc_u[...] += dot(x, up[rows, :])

    def expand_direct(n):
        x = xd[:, :, pl.ds(pl.multiple_of(n * width, 128), width)].reshape(ROWS, width)
        rows = pl.ds(pl.multiple_of(planar + n * width, 128), width)
        acc_g[...] += dot(x, gate[rows, :])
        acc_u[...] += dot(x, up[rows, :])

    def gather_step(k):
        q = from_chip(k)
        ag_copy(k, q).wait_recv()
        fw_copy(k, q).start()

    half = direct // width
    gather_step(1)
    loop(0, 4, df_wait)
    expand_direct(0)

    def early(k):
        gather_step(k)
        expand_direct(k - 1)

    def late(k):
        gather_step(k)
        expand(2 * (k - half - 1))
        expand(2 * (k - half - 1) + 1)

    loop(2, half + 1, early)
    loop(half + 1, CHIPS, late)
    loop(2 * (CHIPS - half - 1), CHIPS, expand)
    g = acc_g[...]
    h32 = g / (1.0 + jnp.exp(-g)) * acc_u[...]
    hown[...] = h32.astype(BF16)
    h_copy = remote(hown, hsib, h_sem.at[0], h_sem.at[1], sib)
    h_copy.start()
    ht[...] = jnp.transpose(hown[...].astype(F32)).astype(BF16)
    ht_copy = pltpu.make_async_copy(ht, ht_hbm, ht_sem)
    ht_copy.start()
    pending["ht"] = ht_copy.wait

    def grams(h, base):
        for f in range(2):
            hf = h[:, f * 128:(f + 1) * 128]
            gram[base + f] = packed(FACTOR * FACTOR * dot(hf, hf, 1, 1))

    grams(hown[...], 0)
    pending.pop("v")()
    pending.pop("k")()
    h_copy.wait()
    grams(hsib[...], 2)

    def masked(v, k0, k1):
        return jnp.concatenate([v[:128] * (1.0 - k0).astype(BF16), v[128:] * (1.0 - k1).astype(BF16)], axis=0)

    def av_copy(k, q):
        return remote(stage.at[q, pl.ds(PACKED + 128, 128)], av.at[p], av_ssem.at[k], av_rsem.at[k], (e, 2 * q + c))

    def partial(q):
        j = 2 * q + c
        ko = [kb[f, pl.ds(j, 1), :] for f in range(2)]
        ks = [ksib[f, pl.ds(j, 1), :] for f in range(2)]
        stage[q, 0:PACKED] = (ko[0] * gram[0] + ko[1] * gram[1] + ks[0] * gram[2] + ks[1] * gram[3]).astype(BF16)
        vo = down[:, pl.ds(pl.multiple_of(j * 128, 128), 128)]
        vs = vsib[q]
        both = dot(hown[...], jnp.concatenate([masked(vo, *ko), vo], axis=1))
        both += dot(hsib[...], jnp.concatenate([masked(vs, *ks), vs], axis=1))
        both = (FACTOR * both).astype(BF16)
        stage[q, PACKED:PACKED + 128] = both[:, :128]
        stage[q, PACKED + 128:] = both[:, 128:]

    def across(dy, dx):
        return 4 * lax.rem(p // 4 + dy, 4) + lax.rem(lax.rem(p, 4) + dx, 4)

    def first(way, far, step):
        q = across(far, step) if way == 0 else across(step, far)
        to = across(0, step) if way == 0 else across(step, 0)
        i = 4 * (step - 1) + far
        return remote(stage.at[q, pl.ds(way * HALF, HALF)], one.at[way, i], one_ssem.at[way, i], one_rsem.at[way, i], (e, 2 * to + c))

    def second(way, far):
        to = across(far, 0) if way == 0 else across(0, far)
        return remote(relay.at[way, far - 1], two.at[way, far - 1], two_ssem.at[way, far - 1], two_rsem.at[way, far - 1], (e, 2 * to + c))

    def send_far(n):
        dy, dx = n // 3 + 1, lax.rem(n, 3) + 1
        partial(across(dy, dx))
        first(0, dy, dx).start()
        first(1, dx, dy).start()

    def send_near(d):
        partial(across(0, d))
        first(0, 0, d).start()
        partial(across(d, 0))
        first(1, 0, d).start()

    loop(0, 9, send_far)
    loop(1, 4, send_near)
    partial(p)

    def firsts_sent(n):
        far, step = lax.rem(n, 4), n // 4 + 1
        first(0, far, step).wait_send()
        first(1, far, step).wait_send()

    pending["one"] = lambda: loop(0, 12, firsts_sent)

    def gathered(way, far):
        q = across(far, 0) if way == 0 else across(0, far)
        total = stage[q, way * HALF:(way + 1) * HALF].astype(F32)
        for step in range(1, 4):
            first(way, far, step).wait_recv()
            total += one[way, 4 * (step - 1) + far].astype(F32)
        return total

    for far in range(1, 4):
        for way in range(2):
            relay[way, far - 1] = gathered(way, far).astype(BF16)
            second(way, far).start()

    pending["two"] = lambda: [second(way, far).wait_send() for way in range(2) for far in range(1, 4)]
    halves = [gathered(way, 0) for way in range(2)]
    for far in range(1, 4):
        for way in range(2):
            second(way, far).wait_recv()
            halves[way] += two[way, far - 1].astype(F32)

    summed = jnp.concatenate(halves, axis=0)
    big, r0 = unpacked(summed[:PACKED]), summed[PACKED:]

    def av_in(k, q):
        return remote(stage.at[p, pl.ds(PACKED + 128, 128)], av.at[q], av_ssem.at[k], av_rsem.at[k], (e, 2 * q + c))


    eye = lax.broadcasted_iota(jnp.int32, (128, 128), 0) == lax.broadcasted_iota(jnp.int32, (128, 128), 1)
    scale = jnp.sum(jnp.sum(jnp.where(eye, big, 0.0), axis=0, keepdims=True), axis=1, keepdims=True)
    scale = jnp.maximum(scale, TINY)
    mb = (big / scale).astype(BF16)

    def apply(v):
        hi = v.astype(BF16)
        lo = (v - hi.astype(F32)).astype(BF16)
        w = dot(mb, jnp.concatenate([hi, lo], axis=1))
        return w[:, :128] + w[:, 128:]

    v1 = apply(r0)
    v2 = apply(v1)
    v3 = apply(v2)

    def inner(a, b):
        return jnp.sum(a * b, axis=0, keepdims=True)

    tiles[s] = jnp.concatenate(
        [inner(r0, v1), inner(v1, v1), inner(v1, v2), inner(v2, v2), inner(v2, v3), inner(v3, v3),
         jnp.broadcast_to(scale, (1, 128)), jnp.zeros((1, 128), F32)], axis=0)

    def t_copy(k, src):
        return remote(tiles.at[src], tiles.at[src], t_ssem.at[k], t_rsem.at[k], (e, lax.rem(s + k, SHARDS)))

    loop(1, SHARDS, lambda k: t_copy(k, s).start())
    loop(1, CHIPS, lambda k: av_copy(k, chip(k)).start())
    pending["av"] = lambda: loop(1, CHIPS, lambda k: av_copy(k, chip(k)).wait_send())
    pending["av in"] = lambda: loop(1, CHIPS, lambda k: av_in(k, from_chip(k)).wait_recv())
    pending["t"] = lambda: loop(1, SHARDS, lambda k: t_copy(k, s).wait_send())
    loop(1, SHARDS, lambda k: t_copy(k, lax.rem(s + SHARDS - k, SHARDS)).wait_recv())

    every = tiles[...]
    scales = every[:, 6:7, :]
    top = jnp.max(scales, axis=0, keepdims=True)
    ratio = jnp.broadcast_to(scales / top, every.shape)
    which = lax.broadcasted_iota(jnp.int32, every.shape, 1)
    power = ratio
    weight = jnp.where(which == 0, power, 0.0)
    for k in range(1, 6):
        power = power * ratio
        weight = jnp.where(which == k, power, weight)
    moments = jnp.sum(jnp.sum(every * weight, axis=0), axis=1, keepdims=True)
    m = [None] + [moments[k:k + 1] for k in range(6)]
    top = top[0, :, 0:1]
    coef = step_scalars(m, EPS / top, EPS / top / top)
    rel = scale / top
    coef = [coef[0], coef[1] * rel, coef[2] * rel * rel]
    total = coef[0] * r0 + coef[1] * v1 + coef[2] * v2
    mine[...] = (FACTOR / top * total).astype(BF16)

    own_copy = pltpu.make_async_copy(mine, sg.at[p, c], own_sem)
    own_copy.start()

    def s_copy(k):
        return remote(mine, sg.at[p, c], s_ssem.at[k], s_rsem.at[k], (e, 2 * chip(k) + c))

    def s_in(k, q):
        return remote(mine, sg.at[q, c], s_ssem.at[k], s_rsem.at[k], (e, 2 * chip(k) + c))

    def sf_copy(k, q):
        return remote(sg.at[q, c], sg.at[q, c], sf_ssem.at[k], sf_rsem.at[k], sib)

    def sf_wait(k, q):
        remote(sg.at[q, 1 - c], sg.at[q, 1 - c], sf_ssem.at[k], sf_rsem.at[k], sib).wait_recv()

    own_share = remote(mine, sg.at[p, c], sf_ssem.at[0], sf_rsem.at[0], sib)
    own_share.start()
    loop(1, CHIPS, lambda k: s_copy(k).start())
    pending["s"] = lambda: loop(1, CHIPS, lambda k: s_copy(k).wait_send())
    pending["sf"] = lambda: (own_share.wait_send(), loop(1, CHIPS, lambda k: sf_copy(k, from_chip(k)).wait_send()))
    pending["own"] = own_copy.wait

    last = r0 - rel * (coef[0] * v1 + coef[1] * v2 + coef[2] * v3)

    def add_av(k, carry):
        q = from_chip(k)
        av_in(k, q).wait_recv()
        return carry + av[q].astype(F32)

    pending.pop("av in")
    whole = lax.fori_loop(1, CHIPS, add_av, stage[p, PACKED + 128:].astype(F32))
    fit[...] = (whole - last).astype(BF16)
    returns = []
    for at, d in enumerate(ORDER):
        if d:
            back_copy = remote(fit.at[pl.ds(at * CAP, CAP)], ret.at[pl.ds(d * CAP, CAP)], r_ssem.at[d], r_rsem.at[d], (back(d), s))
            back_copy.start()
            returns.append(back_copy)
        else:
            ret[0:CAP] = fit[at * CAP:(at + 1) * CAP]

    def share_step(k):
        q = from_chip(k)
        s_in(k, q).wait_recv()
        sf_copy(k, q).start()

    loop(1, 12, share_step)
    for back_copy in returns:
        back_copy.wait()
    refitted[...] = lax.dot_general(combining, ret[...].astype(F32), (((0,), (0,)), ((), ())),
                                    precision=lax.Precision.HIGHEST, preferred_element_type=F32).astype(BF16)
    refit_copy = pltpu.make_async_copy(refitted, refit_hbm, refit_sem)
    refit_copy.start()
    loop(12, CHIPS, share_step)
    loop(0, CHIPS, lambda k: sf_wait(k, from_chip(k)))
    refit_copy.wait()
    finish()


PIECES = 4


def apply_kernel(sg_hbm, ht_hbm, refit_hbm, down_hbm, kept_hbm, refit_ref, new_hbm, sg, ht, down, kept, new, sem, out_sem):
    wide = DW // PIECES
    chips = CHIPS // PIECES

    def cols(i):
        return pl.ds(i * wide, wide)

    small = [pltpu.make_async_copy(a, b, sem.at[i]) for i, (a, b) in enumerate([(ht_hbm, ht), (kept_hbm, kept), (refit_hbm, refit_ref)])]
    parts = []
    for i in range(PIECES):
        parts.append((
            pltpu.make_async_copy(sg_hbm.at[pl.ds(i * chips, chips)], sg.at[pl.ds(i * chips, chips)], sem.at[3 + 2 * i]),
            pltpu.make_async_copy(down_hbm.at[0, :, cols(i)], down.at[:, cols(i)], sem.at[4 + 2 * i])))
    for copy in small[:2] + [copy for part in parts for copy in part] + small[2:]:
        copy.start()
    small[0].wait()
    small[1].wait()
    h = ht[...]
    row = lax.broadcasted_iota(jnp.int32, (2, 128), 0)
    keeps = [dot(kept[0].astype(F32), (row == f).astype(F32), 0, 0) for f in range(2)]
    writes = []
    for i in range(PIECES):
        for copy in parts[i]:
            copy.wait()
        for n in range(2 * chips):
            j = 2 * chips * i + n
            at = slice(j * 128, (j + 1) * 128)
            w = dot(h, sg[j // 2, j % 2]) + down[:, at].astype(F32)
            new[:128, at] = (w[:128] * keeps[0][j:j + 1]).astype(BF16)
            new[128:, at] = (w[128:] * keeps[1][j:j + 1]).astype(BF16)
        write = pltpu.make_async_copy(new.at[:, cols(i)], new_hbm.at[0, :, cols(i)], out_sem.at[i])
        write.start()
        writes.append(write)
    for copy in writes + small[2:]:
        copy.wait()


def body(tokens, routes, router_logits, gate_weight, up_weight, down_weight, kept_blocks):
    rows, model = tokens.shape
    width = model * 2 // (3 * CHIPS)
    direct = model // 3
    own = gate_weight.shape[2]
    dma = pltpu.SemaphoreType.DMA
    vmem = pl.BlockSpec(memory_space=pltpu.VMEM)
    hbm = pl.BlockSpec(memory_space=pltpu.HBM)
    gathered, turned, refit = pl.pallas_call(
        kernel,
        out_shape=(jax.ShapeDtypeStruct((CHIPS, 2, 128, 128), BF16), jax.ShapeDtypeStruct((own, ROWS), BF16),
                   jax.ShapeDtypeStruct((rows, DW // SHARDS), BF16)),
        in_specs=[hbm] * 7,
        out_specs=(hbm, hbm, hbm),
        scratch_shapes=[
            pltpu.VMEM((rows, width), BF16),
            pltpu.VMEM((rows, direct), BF16),
            pltpu.VMEM((2, rows), jnp.int32),
            pltpu.VMEM((2, rows), F32),
            pltpu.VMEM(kept_blocks.shape, jnp.int32),
            pltpu.VMEM((model, own), BF16),
            pltpu.VMEM((model, own), BF16),
            pltpu.VMEM((own, DW), BF16),
            pltpu.VMEM((ROWS, width), BF16),
            pltpu.VMEM((ROWS, direct), BF16),
            pltpu.VMEM((CHIPS, 2, ROWS // 2, width), BF16),
            pltpu.VMEM((2, ROWS // 2, direct), BF16),
            pltpu.VMEM((ROWS, own), F32),
            pltpu.VMEM((ROWS, own), F32),
            pltpu.VMEM((ROWS, own), BF16),
            pltpu.VMEM((ROWS, own), BF16),
            pltpu.VMEM((own, ROWS), BF16),
            pltpu.VMEM((CHIPS, own, 128), BF16),
            pltpu.VMEM((2, SHARDS, 128), F32),
            pltpu.VMEM((2, SHARDS, 128), F32),
            pltpu.VMEM((4, PACKED, 128), F32),
            pltpu.VMEM((CHIPS, PACKED + 256, 128), BF16),
            pltpu.VMEM((2, 12, HALF, 128), BF16),
            pltpu.VMEM((2, 3, HALF, 128), BF16),
            pltpu.VMEM((2, 3, HALF, 128), BF16),
            pltpu.VMEM((CHIPS, 128, 128), BF16),
            pltpu.VMEM((SHARDS, 8, 128), F32),
            pltpu.VMEM((ROWS, 128), BF16),
            pltpu.VMEM((ROWS, 128), BF16),
            pltpu.VMEM((ROWS, 128), BF16),
            pltpu.VMEM((rows, DW // SHARDS), BF16),
            dma((8,)),
            dma((4,)), dma((4,)),
            dma((4,)), dma((4,)),
            dma((4,)), dma((4,)),
            dma((CHIPS,)), dma((CHIPS,)),
            dma((CHIPS,)), dma((CHIPS,)),
            dma((CHIPS,)), dma((CHIPS,)),
            dma((2,)), dma((2,)),
            dma((2, 12)), dma((2, 12)),
            dma((2, 3)), dma((2, 3)),
            dma((CHIPS,)), dma((CHIPS,)),
            dma((SHARDS,)), dma((SHARDS,)),
            dma((CHIPS,)), dma((CHIPS,)),
            dma((CHIPS,)), dma((CHIPS,)),
            dma((GROUPS,)), dma((GROUPS,)),
            dma, dma, dma,
        ],
        compiler_params=pltpu.CompilerParams(collective_id=0, has_side_effects=True, vmem_limit_bytes=60 << 20),
        name="refit",
    )(tokens, routes.T, router_logits.T, gate_weight, up_weight, down_weight, kept_blocks)
    return pl.pallas_call(
        apply_kernel,
        out_shape=(jax.ShapeDtypeStruct(refit.shape, BF16), jax.ShapeDtypeStruct(down_weight.shape, BF16)),
        in_specs=[hbm] * 5,
        out_specs=(vmem, hbm),
        scratch_shapes=[
            pltpu.VMEM(gathered.shape, BF16),
            pltpu.VMEM(turned.shape, BF16),
            pltpu.VMEM((own, DW), BF16),
            pltpu.VMEM(kept_blocks.shape, jnp.int32),
            pltpu.VMEM((own, DW), BF16),
            dma((3 + 2 * PIECES,)),
            dma((PIECES,)),
        ],
        compiler_params=pltpu.CompilerParams(vmem_limit_bytes=60 << 20),
        name="apply",
    )(gathered, turned, refit, down_weight, kept_blocks)


def solution(mesh):
    in_specs = (
        P("expert", None),
        P("expert", None),
        P("expert", None),
        P("expert", None, "shard"),
        P("expert", None, "shard"),
        P("expert", "shard", None),
        P("expert", "shard", None),
    )
    out_specs = (P("expert", "shard"), P("expert", "shard", None))
    return jax.shard_map(body, mesh=mesh, in_specs=in_specs, out_specs=out_specs, check_vma=False)
```
